256 devices in a mesh: tower: 8 (over x, core), peer: 32 (over z, y).
Axes of the slice: x: 4, y: 4, z: 8, core: 2. Of those that a mesh axis runs over, the one named last changes fastest.
Arguments:
- embeddings: bfloat16 [16384, 2048], P('tower', 'peer'), may hold values from -6 to 6
- session_lists: int32 [8, 2048], P('tower'), may hold values from 0 to 2047, each once within a row
- owners: int32 [16384, 1], P(('tower', 'peer')), may hold values from 0 to 7; in each aligned block of 64 rows (0 to 63, 64 to 127, ...) at most 16 rows name the same one
- counts: int32 [16384], P(('tower', 'peer')), may hold values from 1 to 3, as said below
- item_feats: bfloat16 [98304, 256], P(('tower', 'peer')), may hold values from -6 to 6
- cotangent: bfloat16 [98304, 1024], P(('tower', 'peer')), may hold values from -6 to 6
- cross_down: bfloat16 [2048, 256], replicated, may hold values from -0.125 to 0.125
- cross_up: bfloat16 [256, 2048], replicated, may hold values from -0.375 to 0.375
- compress: bfloat16 [2048, 256], replicated, may hold values from -0.125 to 0.125
- over_first: bfloat16 [512, 4096], replicated, may hold values from -0.25 to 0.25
- over_second: bfloat16 [4096, 1024], P('peer'), may hold values from -0.09375 to 0.09375
- over_third: bfloat16 [1024, 1024], replicated, may hold values from -0.1875 to 0.1875
Outputs:
- over_out: bfloat16 [98304, 1024], P(('tower', 'peer'))
- emb_grad: bfloat16 [16384, 2048], P('tower', 'peer')
The draws below stay inside these ranges and needn't reach their ends.
Inputs may be any that keep to these rules, and one draw needn't show every extreme that they name: `session_lists`: each row is a permutation of the tower's 64 * 32 table rows. `owners`: within the 64 sessions of one device, no tower owns more than 16 of them. `counts`: the first session of every device has 3 samples and the second has one.
All inputs are finite; a program needn't handle non-finite values.
Results may differ from the reference program's by a relative error of at most 0.02.
Values may be sent and summed in bfloat16 or wider, within the bound.
A program may use at most 128 MiB of HBM per device.

```python
import math
import jax
import jax.numpy as jnp
import numpy as np
from jax import lax

FEAT = 2048
RANK = 256
COMP = 256
ITEM = 256
H1 = 4096
H2 = 1024
H3 = 1024
U_DEV = 64
MOSTC = 3
CAP = 16
SESSIONS = 16384
GRID = 98304
N_TOWER = 8
N_PEER = 32


def draw_counts(key, part):
    values = jax.random.randint(key, (SESSIONS,), 1, MOSTC + 1, dtype=jnp.int32)
    position = jnp.arange(SESSIONS, dtype=jnp.int32) % U_DEV
    values = jnp.where(position == 0, MOSTC, values)
    values = jnp.where(position == 1, 1, values)
    return values.astype(jnp.int32)


def block_scale(rng, dims, cuts, least, high):
    def one(axis_at, shards_of):
        heights = jax.random.uniform(jax.random.fold_in(jax.random.fold_in(rng, 6), axis_at), (shards_of,), jnp.float32, least / len(cuts), high / len(cuts))
        return jnp.repeat(jnp.exp(heights), dims[axis_at] // shards_of).reshape((-1,) + (1,) * (len(dims) - axis_at - 1))

    loudness = one(*cuts[0])
    for cut in cuts[1:]:
        loudness = loudness * one(*cut)
    return loudness


def assign_block(rng, own, number, rows, count, top, most, skew):
    ranking = jax.random.permutation(rng, count)
    crowded, ordinary = load_shares(count, rows * top, most, skew, True), load_shares(count, rows * top, most, skew, False)
    places = jnp.arange(count)

    def named(sizes, offset_by):
        used = int((sizes > 0).sum())
        fixed = max(1, used // 4)
        moved = fixed + (places - fixed + offset_by * (used - fixed)) % max(1, count - fixed)
        return jnp.zeros((count,), jnp.int32).at[ranking[jnp.where(places < fixed, places, moved)]].set(jnp.asarray(sizes, jnp.int32))

    sizes = jnp.where(number % 4 == 0, named(crowded, number // 4), named(ordinary, number - number // 4 - 1))
    mixed = jax.random.permutation(jax.random.fold_in(own, 3), count)
    donor, taker = mixed[0:count // 2 * 2:2], mixed[1:count // 2 * 2:2]
    room = jnp.minimum(sizes[donor] - 1, most - sizes[taker]) // 2
    room = jnp.where((donor == ranking[0]) | (taker == ranking[0]) | (sizes[taker] == 0), 0, jnp.maximum(room, 0))
    moved = jax.random.randint(jax.random.fold_in(own, 4), (count // 2,), 0, 1 << 20) % (room + 1)
    sizes = sizes.at[donor].add(-moved).at[taker].add(moved)
    items = jnp.searchsorted(jnp.cumsum(sizes), jnp.arange(rows * top), side="right").astype(jnp.int32)
    grid = items.reshape(top, rows).T
    grid = grid[jax.random.permutation(jax.random.fold_in(own, 1), rows)]
    offset_by = jax.random.randint(jax.random.fold_in(own, 2), (rows, 1), 0, top)
    return jnp.take_along_axis(grid, (jnp.arange(top)[None, :] + offset_by) % top, axis=1)


def load_shares(count, total, reach, skew, full):
    portions = [(1 << 20) // math.isqrt(rank ** skew) + 1 for rank in range(1, count + 1)]
    largest = reach if full else min(reach, max(-(-total // count), total * portions[0] // sum(portions)))
    least = 1 if total - largest >= count - 1 else 0
    holding, rest = [largest] + [least] * (count - 1), total - largest - least * (count - 1)
    while rest > 0:
        candidates = [i for i in range(1, count) if holding[i] < largest] or [i for i in range(1, count) if holding[i] < reach]
        whole, budget = sum([portions[i] for i in candidates]), rest
        for i in candidates:
            more = min(reach - holding[i], max(1, budget * portions[i] // whole), rest)
            holding[i] = holding[i] + more
            rest = rest - more
    return np.array(holding)


def noise(own_key, dims, spread, limit, split=(), kind=jnp.bfloat16):
    drawn = spread * jax.random.normal(own_key, dims, jnp.float32)
    if split:
        drawn = drawn * block_scale(own_key, dims, split, -0.22, 0.18)
    return jnp.clip(drawn, -limit, limit).astype(kind)


def setup_inputs(seed: int = 0) -> dict:
    arg_keys = jax.random.split(jax.random.key(seed), 13)
    embeddings = noise(arg_keys[0], (SESSIONS, FEAT), 1.0, 6.0, ((0, 8), (1, 32)))
    session_lists = jax.vmap(lambda own: jax.random.permutation(own, U_DEV * N_PEER))(jax.random.split(arg_keys[1], N_TOWER)).reshape((N_TOWER, U_DEV * N_PEER)).astype(jnp.int32)
    owners_keys = jax.random.split(jax.random.fold_in(arg_keys[2], 1), SESSIONS // U_DEV)
    owners_turns = jax.random.permutation(jax.random.fold_in(arg_keys[2], 3), SESSIONS // U_DEV)
    owners = jax.vmap(lambda own, number: assign_block(jax.random.fold_in(arg_keys[2], 2), own, number, U_DEV, N_TOWER, 1, CAP, 2))(owners_keys, owners_turns).reshape((SESSIONS, 1))
    counts = draw_counts(jax.random.fold_in(arg_keys[12], 71), 0)
    item_feats = noise(arg_keys[4], (GRID, ITEM), 1.0, 6.0, ((0, 256),))
    cotangent = noise(arg_keys[5], (GRID, H3), 1.0, 6.0, ((0, 256),))
    cross_down = noise(arg_keys[6], (FEAT, RANK), FEAT ** -0.5, 0.125)
    cross_up = noise(arg_keys[7], (RANK, FEAT), RANK ** -0.5, 0.375)
    compress = noise(arg_keys[8], (FEAT, COMP), FEAT ** -0.5, 0.125)
    over_first = noise(arg_keys[9], (COMP + ITEM, H1), (COMP + ITEM) ** -0.5, 0.25)
    over_second = noise(arg_keys[10], (H1, H2), H1 ** -0.5, 0.09375, ((0, 32),))
    over_third = noise(arg_keys[11], (H2, H3), H2 ** -0.5, 0.1875)
    return {"embeddings": embeddings, "session_lists": session_lists, "owners": owners, "counts": counts, "item_feats": item_feats, "cotangent": cotangent, "cross_down": cross_down, "cross_up": cross_up, "compress": compress, "over_first": over_first, "over_second": over_second, "over_third": over_third}


def silu_slope(pre):
    sigma = jax.nn.sigmoid(pre)
    return sigma * (1.0 + pre * (1.0 - sigma))


def times_t(left, right):
    return lax.dot_general(left, right, (((1,), (1,)), ((), ())), preferred_element_type=jnp.float32)


def reference(embeddings, session_lists, owners, counts, item_feats, cotangent, cross_down, cross_up, compress, over_first, over_second, over_third):
    tower_rows = U_DEV * N_PEER
    devices_all = N_TOWER * N_PEER
    slot_total = N_TOWER * CAP
    offsets = jnp.arange(N_TOWER, dtype=jnp.int32)[:, None] * tower_rows
    source_rows = (session_lists.astype(jnp.int32) + offsets).reshape(-1)
    session_rows = embeddings[source_rows]
    low = jnp.dot(session_rows, cross_down, preferred_element_type=jnp.float32).astype(jnp.bfloat16)
    lift = jnp.dot(low, cross_up, preferred_element_type=jnp.float32)
    rows_wide = session_rows.astype(jnp.float32)
    crossed = (rows_wide * lift + rows_wide).astype(jnp.bfloat16)
    compressed = jnp.dot(crossed, compress, preferred_element_type=jnp.float32).astype(jnp.bfloat16)

    owner_blocks = owners[:, 0].astype(jnp.int32).reshape(devices_all, U_DEV)
    choose = (owner_blocks[:, :, None] == jnp.arange(N_TOWER, dtype=jnp.int32)[None, None, :]).astype(jnp.int32)
    earlier = jnp.cumsum(choose, axis=1) - choose
    position = jnp.sum(choose * earlier, axis=2)
    device_ids = jnp.arange(devices_all, dtype=jnp.int32)
    source_tower = device_ids // N_PEER
    source_peer = device_ids % N_PEER
    receiver = owner_blocks * N_PEER + source_peer[:, None]
    slot = source_tower[:, None] * CAP + position
    flat_target = (receiver * slot_total + slot).reshape(-1).astype(jnp.int32)
    received = jnp.zeros((devices_all * slot_total, COMP), jnp.bfloat16).at[flat_target].set(compressed)
    slot_counts = jnp.zeros((devices_all * slot_total,), jnp.int32).at[flat_target].set(counts.astype(jnp.int32))

    live = (jnp.arange(MOSTC, dtype=jnp.int32)[None, :] < slot_counts[:, None]).astype(jnp.float32)
    live = live.reshape(devices_all, slot_total * MOSTC)
    expanded = jnp.broadcast_to(received[:, None, :], (devices_all * slot_total, MOSTC, COMP))
    expanded = expanded.reshape(devices_all, slot_total * MOSTC, COMP)

    def over_arch(pieces):
        rows_in, items, grads_in, mask = pieces
        inputs = jnp.concatenate([rows_in, items], axis=1)
        pre_first = jnp.dot(inputs, over_first, preferred_element_type=jnp.float32)
        hidden_first = jax.nn.silu(pre_first).astype(jnp.bfloat16)
        pre_second = jnp.dot(hidden_first, over_second, preferred_element_type=jnp.float32)
        hidden_second = jax.nn.silu(pre_second).astype(jnp.bfloat16)
        result = (jnp.dot(hidden_second, over_third, preferred_element_type=jnp.float32) * mask[:, None]).astype(jnp.bfloat16)
        masked = grads_in * mask[:, None].astype(jnp.bfloat16)
        grad_second = (times_t(masked, over_third) * silu_slope(pre_second)).astype(jnp.bfloat16)
        grad_first = (times_t(grad_second, over_second) * silu_slope(pre_first)).astype(jnp.bfloat16)
        sample_grad = times_t(grad_first, over_first[:COMP]).astype(jnp.bfloat16)
        slot_grad = jnp.sum(sample_grad.astype(jnp.float32).reshape(slot_total, MOSTC, COMP), axis=1).astype(jnp.bfloat16)
        return result, slot_grad

    over_out, slot_grads = lax.map(over_arch, (expanded, item_feats.reshape(devices_all, slot_total * MOSTC, ITEM), cotangent.reshape(devices_all, slot_total * MOSTC, H3), live))
    session_grad = slot_grads.reshape(devices_all * slot_total, COMP)[flat_target]
    grad_crossed = times_t(session_grad, compress).astype(jnp.bfloat16)
    grad_lift = (grad_crossed.astype(jnp.float32) * rows_wide).astype(jnp.bfloat16)
    grad_low = times_t(grad_lift, cross_up).astype(jnp.bfloat16)
    grad_rows = (grad_crossed.astype(jnp.float32) * (lift + 1.0) + times_t(grad_low, cross_down)).astype(jnp.bfloat16)
    emb_grad = jnp.zeros_like(embeddings).at[source_rows].set(grad_rows)
    return over_out.reshape(devices_all * slot_total * MOSTC, H3), emb_grad
```

```python
import jax
import jax.numpy as jnp
from jax import lax
from jax.experimental import pallas as pl
from jax.experimental.pallas import tpu as pltpu
from jax.sharding import PartitionSpec as P

MESH = pl.DeviceIdType.MESH
F32 = jnp.float32
BF16 = jnp.bfloat16
NX, NC, NY, NZ = 4, 2, 4, 8
NP, NT = NY * NZ, NX * NC
ROWS, SLOTS, MOSTC, CAP = 384, 128, 3, 16
UDEV = 64
FEAT, WIDE = 2048, 256
H1, H2 = 4096, 1024
HZ = H1 // NZ
HS = H1 // NP
LISTED = UDEV * NP
FOLD = 4
RBLK = LISTED // FOLD
ZREL = (0, 7, 1, 6, 2, 5, 3, 4)
BATCH = ((0, 1), (1, 2), (3, 2), (5, 3))


def dot(a, b):
    return jnp.dot(a, b, preferred_element_type=F32)


def dot_t(a, b):
    return lax.dot_general(a, b, (((1,), (1,)), ((), ())), preferred_element_type=F32)


def wrap(v, n):
    return lax.rem(v + 2 * n, n)


def iota(shape, axis):
    return lax.broadcasted_iota(jnp.int32, shape, axis)


def kernel(
    emb, lists, owners, counts, item, cot, cd, cu, comp, of, w2, ot,
    out_hbm, eg_hbm,
    embv, listv, ownv, cntv, itemv, cotv, cdv, cuv, compv, ofv, W2, otv,
    hot, pay, arr, SR, lift, tsend, trecv, gsend, grecv, bpay, barr, egv,
    prei, hid, slope, pre2, g3, hs, gs2, outv, sacc,
    lsem, asend, arecv, tsem, trsem, gsem, grsem, bsend, brecv,
    zs, zr, ys, yr, xs, xr, ds, dr,
):
    t = lax.axis_index("tower")
    p = lax.axis_index("peer")
    x, c = t // NC, t % NC
    y, z = p % NY, p // NY
    px = x % 2
    c64 = c * 64

    def peer_at(dz, dy):
        return (t, wrap(z + dz, NZ) * NY + wrap(y + dy, NY))

    def far_first(i):
        a, b = i // NY, i % NY
        ka, kb = (a + 1) // 2, (b + 1) // 2
        dz = NZ // 2 + ka * (1 - 2 * (a % 2))
        dy = NY // 2 + kb * (1 - 2 * (b % 2))
        return dz, dy

    loads = [
        (emb, embv), (lists, listv), (w2, W2.at[0, y]), (owners, ownv), (counts, cntv), (item, itemv),
    ]
    for s in range(NZ):
        zz = wrap(z + ZREL[s], NZ)
        loads.append((of.at[:, pl.ds(pl.multiple_of(zz * HZ, HZ), HZ)], ofv.at[s]))
    loads += [(cot, cotv), (ot, otv), (cd, cdv), (cu, cuv), (comp, compv)]
    copies = [pltpu.make_async_copy(a, b, lsem.at[i]) for i, (a, b) in enumerate(loads)]
    for cp in copies:
        cp.start()
    L_EMB, L_LIST, L_W2, L_OWN, L_CNT, L_ITEM, L_OF = 0, 1, 2, 3, 4, 5, 6
    L_COT, L_OT, L_CD, L_CU, L_COMP = 14, 15, 16, 17, 18

    barrier = pltpu.get_barrier_semaphore()

    def greet_peer(i, carry):
        dz, dy = far_first(i)
        pl.semaphore_signal(barrier, inc=1, device_id=peer_at(dz, dy), device_id_type=MESH)
        return carry

    lax.fori_loop(0, NP - 1, greet_peer, 0)

    def greet_tower(i, carry):
        pl.semaphore_signal(barrier, inc=1, device_id=(wrap(t + i, NT), p), device_id_type=MESH)
        return carry

    lax.fori_loop(1, NT, greet_tower, 0)

    copies[L_EMB].wait()
    copies[L_LIST].wait()
    order = listv[...]
    inner = order & (RBLK - 1)
    quarter = order >> 9
    lane = iota((32, 128), 1)

    def build_hot(k, carry):
        r0 = pl.multiple_of(k * 64, 64)
        rows = iota((64, LISTED), 0) + r0
        hot[pl.ds(r0, 64), :] = jnp.where(rows == inner, 1.0, 0.0).astype(BF16)
        return carry

    lax.fori_loop(0, RBLK // 64, build_hot, 0)
    stacked = jnp.concatenate([embv[:, k * RBLK:(k + 1) * RBLK] for k in range(FOLD)], axis=0)
    for n in range(4):
        cols = slice(n * 512, (n + 1) * 512)
        got = dot(stacked, hot[:, cols])
        q = quarter[:, cols]
        srt = jnp.where(q == 0, got[0:64], 0.0)
        for k in range(1, FOLD):
            srt = srt + jnp.where(q == k, got[k * 64:(k + 1) * 64], 0.0)
        for b in range(4):
            blk = srt[:, b * 128:(b + 1) * 128]
            both = jnp.concatenate([blk, pltpu.roll(blk, 96, 1)], axis=0)
            turned = both.T.astype(BF16)
            pay[n * 8 + b * 2] = turned[0:32]
            pay[n * 8 + b * 2 + 1] = turned[64:96]

    pl.semaphore_wait(barrier, NP - 1 + NT - 1)

    def exchange(src, dst, ssem, rsem):
        def one(i, carry):
            dz, dy = far_first(i)
            to = peer_at(dz, dy)
            pltpu.make_async_remote_copy(
                src_ref=src.at[to[1]], dst_ref=dst.at[p], send_sem=ssem, recv_sem=rsem,
                device_id=to, device_id_type=MESH,
            ).start()
            return carry

        lax.fori_loop(0, NP - 1, one, 0)
        dst[p] = src[p]

    def exchange_wait(dst, sem):
        part = dst.at[pl.ds(0, NP - 1)]
        pltpu.make_async_copy(part, part, sem).wait()

    def towers(src, dst, ssem, rsem):
        for i in range(1, NT):
            to = wrap(t + i, NT)
            pltpu.make_async_remote_copy(
                src_ref=src.at[pl.ds(pl.multiple_of(to * CAP, CAP), CAP)],
                dst_ref=dst.at[pl.ds(pl.multiple_of(t * CAP, CAP), CAP)],
                send_sem=ssem, recv_sem=rsem, device_id=(to, p), device_id_type=MESH,
            ).start()
        mine = pl.ds(pl.multiple_of(t * CAP, CAP), CAP)
        dst[mine] = src[mine]

    def towers_wait(dst, sem):
        part = dst.at[pl.ds(0, SLOTS - CAP)]
        pltpu.make_async_copy(part, part, sem).wait()

    ym, yp, yq = wrap(y - 1, NY), wrap(y + 1, NY), wrap(y + 2, NY)
    SETS = (ym, yp, yq)
    mine32 = c64 + px * 32
    sent = []

    def rcopy(src, dst, ssem, rsem, to):
        return pltpu.make_async_remote_copy(
            src_ref=src, dst_ref=dst, send_sem=ssem, recv_sem=rsem, device_id=to, device_id_type=MESH
        )

    def rows(slot, yy, r0, n):
        return W2.at[slot, yy, pl.ds(pl.multiple_of(r0, 16), n)]

    def rows_b(b, yy, r0, n):
        s0, k = BATCH[b]
        return W2.at[pl.ds(s0, k), yy, pl.ds(pl.multiple_of(r0, 16), n)]

    def z_copies():
        out = []
        for i, (a, b, r0, n, d) in enumerate((
            (0, 1, 0, 64, 1), (0, 2, 0, 64, -1), (0, 3, 0, 64, 2), (0, 4, 0, 64, -2),
            (3, 5, 0, 64, 1), (4, 6, 0, 64, -1), (3, 7, 0, 32, 2), (4, 7, 32, 32, -2),
        )):
            out.append(rcopy(rows(a, y, c64 + r0, n), rows(b, y, c64 + r0, n), zs.at[i], zr.at[i], peer_at(d, 0)))
        return out

    zc = z_copies()

    def start(cp):
        cp.start()
        sent.append(cp)

    def y1(b):
        part = rows_b(b, y, mine32, 32)
        return [rcopy(part, part, ys.at[b * 4 + i], yr.at[b * 4 + i], peer_at(0, d)) for i, d in enumerate((1, -1))]

    def y2(b):
        lo = rows_b(b, ym, mine32, 16)
        hi = rows_b(b, yp, mine32 + 16, 16)
        return [
            rcopy(lo, lo, ys.at[b * 4 + 2], yr.at[b * 4 + 2], peer_at(0, 1)),
            rcopy(hi, hi, ys.at[b * 4 + 3], yr.at[b * 4 + 3], peer_at(0, -1)),
        ]

    def xc(b, k):
        out = []
        for i, d in enumerate((1, -1)):
            part = rows_b(b, SETS[k], mine32 + 16 * i, 16)
            e = b * 6 + k * 2 + i
            out.append(rcopy(part, part, xs.at[e], xr.at[e], (wrap(x + d, NX) * NC + c, p)))
        return out

    def dc(b, k):
        part = rows_b(b, (SETS + (y,))[k], c64, 64)
        e = b * 4 + k
        return rcopy(part, part, ds.at[e], dr.at[e], (x * NC + 1 - c, p))

    def e1(b):
        for i in ((), (0, 1), (2, 3), (4, 5, 6, 7))[b]:
            zc[i].wait_recv()
        if b == 2:
            for i in (4, 5, 6, 7):
                start(zc[i])
        for cp in y1(b):
            start(cp)
        if b:
            start(dc(b, 3))

    def e2(b):
        for cp in y1(b):
            cp.wait_recv()
        for cp in y2(b):
            start(cp)
        for k in (0, 1):
            for cp in xc(b, k):
                start(cp)

    def e3(b):
        for cp in y2(b):
            cp.wait_recv()
        for cp in xc(b, 2):
            start(cp)

    def e4(b, ks):
        for k in ks:
            for cp in xc(b, k):
                cp.wait_recv()
            start(dc(b, k))

    def e5(b):
        for k in ((0, 1, 2) if b == 0 else (0, 1, 2, 3)):
            dc(b, k).wait_recv()

    exchange(pay, arr, asend, arecv)
    copies[L_W2].wait()
    for i in range(4):
        start(zc[i])
    e1(0)

    copies[L_ITEM].wait()
    for s in range(NZ):
        copies[L_OF + s].wait()

    def item_step(s, carry):
        prei[s] = dot(itemv[...], ofv[s, WIDE:, :])
        return carry

    lax.fori_loop(0, NZ, item_step, 0)
    e2(0)
    e1(1)
    e1(2)
    copies[L_COT].wait()
    copies[L_OT].wait()

    def cot_step(n, carry):
        r0 = pl.multiple_of(n * 256, 256)
        g3[:, pl.ds(r0, 256)] = dot_t(cotv[...], otv[pl.ds(r0, 256), :])
        return carry

    lax.fori_loop(0, H2 // 256, cot_step, 0)

    copies[L_OWN].wait()
    copies[L_CNT].wait()
    own = ownv[...]
    choose = jnp.where(iota((8, UDEV), 0) == own, 1.0, 0.0)
    before = jnp.where(iota((UDEV, UDEV), 0) < iota((UDEV, UDEV), 1), 1.0, 0.0).astype(BF16)
    earlier = dot(choose.astype(BF16), before)
    pos = jnp.sum(choose * earlier, axis=0, keepdims=True)
    target = own * CAP + pos.astype(jnp.int32)
    hit = iota((SLOTS, UDEV), 0) == target
    disp = jnp.where(hit, 1.0, 0.0).astype(BF16)
    held = dot(jnp.where(hit, cntv[...].astype(F32), 0.0).astype(BF16), jnp.ones((UDEV, 128), BF16))
    tsend[:, WIDE:] = held.astype(BF16)
    for i in (L_CD, L_CU, L_COMP):
        copies[i].wait()

    exchange_wait(arr, arecv)

    def lay(j, carry):
        a = arr[2 * j].astype(F32)
        b = arr[2 * j + 1].astype(F32)
        at = pl.ds(pl.multiple_of(j * 128, 128), 128)
        SR[0:32, at] = jnp.where(lane < 64, a, pltpu.roll(b, 64, 1)).astype(BF16)
        SR[32:64, at] = jnp.where(lane < 64, pltpu.roll(a, 64, 1), b).astype(BF16)
        return carry

    lax.fori_loop(0, NP // 2, lay, 0)
    low = dot(SR[...], cdv[...]).astype(BF16)
    lift[...] = dot(low, cuv[...])
    wide = SR[...].astype(F32)
    crossed = (wide * lift[...] + wide).astype(BF16)
    compressed = dot(crossed, compv[...]).astype(BF16)
    tsend[:, :WIDE] = dot(disp, compressed).astype(BF16)
    towers(tsend, trecv, tsem, trsem)

    e3(0)
    e2(1)
    e1(3)
    e2(2)
    e4(0, (0, 1, 2))

    towers_wait(trecv, trsem)
    qi = iota((ROWS, SLOTS), 0)
    si = iota((ROWS, SLOTS), 1) * MOSTC
    spread = jnp.where((qi >= si) & (qi < si + MOSTC), 1.0, 0.0).astype(BF16)
    grid = dot(spread, trecv[...])
    expanded = grid[:, :WIDE].astype(BF16)
    third = (qi * 21846) >> 16
    live = jnp.where((qi - third * MOSTC).astype(F32) < grid[:, WIDE:], 1.0, 0.0)[:, 0:1]

    def first_step(s, carry):
        pre = prei[s] + dot(expanded, ofv[s, :WIDE, :])
        sig = 0.5 * jnp.tanh(0.5 * pre) + 0.5
        act = pre * sig
        hid[s] = act.astype(BF16)
        slope[s] = (sig + act * (1.0 - sig)).astype(BF16)
        return carry

    lax.fori_loop(0, NZ, first_step, 0)

    def second(s, n, acc):
        at = pl.ds(pl.multiple_of(n * 256, 256), 256)
        w = W2[s, :, :, at].reshape(HZ, 256)
        v = dot(hid[s], w)
        if acc:
            pre2[:, at] += v
        else:
            pre2[:, at] = v

    def second_slot(s, acc):
        def step(n, carry):
            second(s, n, acc)
            return carry

        lax.fori_loop(0, 4, step, 0)

    e3(1)
    e3(2)
    e4(1, (0, 1, 2))
    e5(0)
    second_slot(0, False)
    e2(3)
    e4(2, (0, 1, 2))
    e5(1)
    second_slot(1, True)
    second_slot(2, True)
    e3(3)
    e5(2)
    second_slot(3, True)
    second_slot(4, True)
    e4(3, (0, 1, 2))
    e5(3)
    for s in (5, 6, 7):
        second_slot(s, True)

    def mid_step(n, carry):
        at = pl.ds(pl.multiple_of(n * 256, 256), 256)
        pre = pre2[:, at]
        sig = 0.5 * jnp.tanh(0.5 * pre) + 0.5
        act = pre * sig
        hs[:, at] = act.astype(BF16)
        gs2[:, at] = (g3[:, at] * live * (sig + act * (1.0 - sig))).astype(BF16)
        return carry

    lax.fori_loop(0, 4, mid_step, 0)
    sacc[...] = jnp.zeros_like(sacc)

    def back_step(s, carry):
        w = W2[s].reshape(HZ, H2)
        g = (dot_t(gs2[...], w) * slope[s].astype(F32)).astype(BF16)
        sacc[...] += dot_t(g, ofv[s, :WIDE, :])
        return carry

    lax.fori_loop(0, NZ, back_step, 0)
    qj = iota((SLOTS, ROWS), 1)
    sj = iota((SLOTS, ROWS), 0) * MOSTC
    gather3 = jnp.where((qj >= sj) & (qj < sj + MOSTC), 1.0, 0.0).astype(BF16)
    gsend[...] = dot(gather3, sacc[...].astype(BF16)).astype(BF16)
    towers(gsend, grecv, gsem, grsem)

    def out_step(n, carry):
        at = pl.ds(pl.multiple_of(n * 256, 256), 256)
        outv[:, at] = (dot(hs[...], otv[:, at]) * live).astype(BF16)
        return carry

    lax.fori_loop(0, 4, out_step, 0)
    out_copy = pltpu.make_async_copy(outv, out_hbm, lsem.at[19])
    out_copy.start()

    towers_wait(grecv, grsem)
    eye = jnp.where(iota((UDEV, UDEV), 0) == iota((UDEV, UDEV), 1), 1.0, 0.0).astype(BF16)
    undisp = dot_t(eye, disp).astype(BF16)
    session_grad = dot(undisp, grecv[...]).astype(BF16)
    gc = dot_t(session_grad, compv[...]).astype(BF16).astype(F32)
    gl = (gc * SR[...].astype(F32)).astype(BF16)
    glow = dot_t(gl, cuv[...]).astype(BF16)
    lift[...] = gc * (lift[...] + 1.0) + dot_t(glow, cdv[...])

    def unlay(j, carry):
        at = pl.ds(pl.multiple_of(j * 128, 128), 128)
        lo = lift[0:32, at]
        hi = lift[32:64, at]
        bpay[2 * j] = jnp.where(lane < 64, lo, pltpu.roll(hi, 64, 1)).astype(BF16)
        bpay[2 * j + 1] = jnp.where(lane < 64, pltpu.roll(lo, 64, 1), hi).astype(BF16)
        return carry

    lax.fori_loop(0, NP // 2, unlay, 0)
    exchange(bpay, barr, bsend, brecv)
    for cp in sent:
        cp.wait_send()
    exchange_wait(pay, asend)
    towers_wait(tsend, tsem)
    towers_wait(gsend, gsem)
    exchange_wait(barr, brecv)

    total = jnp.zeros((FOLD * 64, RBLK), F32)
    zero = jnp.zeros((32, 128), F32)
    lane64 = iota((64, 128), 1) & 63
    for n in range(4):
        parts = []
        for b in range(4):
            p0 = n * 8 + b * 2
            tall = jnp.concatenate([barr[p0].astype(F32), zero, barr[p0 + 1].astype(F32), zero], axis=0)
            turned = tall.T
            parts.append(jnp.where(lane64 < 32, turned[0:64], pltpu.roll(turned[64:128], 32, 1)))
        grads = jnp.concatenate(parts, axis=1)
        q = quarter[:, n * 512:(n + 1) * 512]
        laid = jnp.concatenate([jnp.where(q == k, grads, 0.0).astype(BF16) for k in range(FOLD)], axis=0)
        total = total + dot_t(laid, hot[:, n * 512:(n + 1) * 512])
    for k in range(FOLD):
        egv[:, k * RBLK:(k + 1) * RBLK] = total[k * 64:(k + 1) * 64].astype(BF16)
    eg_copy = pltpu.make_async_copy(egv, eg_hbm, lsem.at[20])
    eg_copy.start()
    exchange_wait(bpay, bsend)
    out_copy.wait()
    eg_copy.wait()


def body(
    embeddings, session_lists, owners, counts, item_feats, cotangent,
    cross_down, cross_up, compress, over_first, over_second, over_third,
):
    dma = pltpu.SemaphoreType.DMA
    vm = pltpu.VMEM
    scratch = [
        vm((64, LISTED), BF16), vm((1, LISTED), jnp.int32), vm((1, UDEV), jnp.int32), vm((1, UDEV), jnp.int32),
        vm((ROWS, WIDE), BF16), vm((ROWS, H2), BF16), vm((FEAT, WIDE), BF16), vm((WIDE, FEAT), BF16),
        vm((FEAT, WIDE), BF16), vm((NZ, 2 * WIDE, HZ), BF16), vm((NZ, NY, HS, H2), BF16), vm((H2, H2), BF16),
        vm((RBLK, LISTED), BF16), vm((NP, 32, 128), BF16), vm((NP, 32, 128), BF16), vm((UDEV, FEAT), BF16),
        vm((UDEV, FEAT), F32), vm((SLOTS, WIDE + 128), BF16), vm((SLOTS, WIDE + 128), BF16),
        vm((SLOTS, WIDE), BF16), vm((SLOTS, WIDE), BF16), vm((NP, 32, 128), BF16), vm((NP, 32, 128), BF16),
        vm((64, LISTED), BF16),
        vm((NZ, ROWS, HZ), F32), vm((NZ, ROWS, HZ), BF16), vm((NZ, ROWS, HZ), BF16), vm((ROWS, H2), F32),
        vm((ROWS, H2), F32), vm((ROWS, H2), BF16), vm((ROWS, H2), BF16), vm((ROWS, H2), BF16), vm((ROWS, WIDE), F32),
        dma((21,)), dma, dma, dma, dma, dma, dma, dma, dma,
        dma((8,)), dma((8,)), dma((16,)), dma((16,)), dma((24,)), dma((24,)), dma((16,)), dma((16,)),
    ]
    anywhere = pl.BlockSpec(memory_space=pl.ANY)
    over_out, emb_grad_t = pl.pallas_call(
        kernel,
        out_shape=(
            jax.ShapeDtypeStruct((ROWS, H2), BF16),
            jax.ShapeDtypeStruct((64, LISTED), BF16),
        ),
        in_specs=[anywhere] * 12,
        out_specs=(anywhere, anywhere),
        scratch_shapes=scratch,
        compiler_params=pltpu.CompilerParams(
            collective_id=0, has_side_effects=True, vmem_limit_bytes=60 * 2**20
        ),
    )(
        embeddings.T, session_lists, owners.reshape(1, UDEV), counts.reshape(1, UDEV), item_feats, cotangent,
        cross_down, cross_up, compress, over_first, over_second, over_third,
    )
    return over_out, emb_grad_t.T


def solution(mesh):
    return jax.shard_map(
        body,
        mesh=mesh,
        in_specs=(
            P("tower", "peer"),
            P("tower", None),
            P(("tower", "peer"), None),
            P(("tower", "peer")),
            P(("tower", "peer"), None),
            P(("tower", "peer"), None),
            P(),
            P(),
            P(),
            P(),
            P("peer", None),
            P(),
        ),
        out_specs=(P(("tower", "peer"), None), P("tower", "peer")),
        check_vma=False,
    )
```

```python
import jax
import jax.numpy as jnp
from jax import lax
from jax.experimental import pallas as pl
from jax.experimental.pallas import tpu as pltpu
from jax.sharding import PartitionSpec as P

MESH = pl.DeviceIdType.MESH
F32 = jnp.float32
BF16 = jnp.bfloat16
NX, NC, NY, NZ = 4, 2, 4, 8
NP, NT = NY * NZ, NX * NC
ROWS, SLOTS, MOSTC, CAP = 384, 128, 3, 16
UDEV = 64
FEAT, WIDE = 2048, 256
H1, H2 = 4096, 1024
HZ = H1 // NZ
HS = H1 // NP
LISTED = UDEV * NP
FOLD = 4
RBLK = LISTED // FOLD
ZREL = (0, 4, 7, 1, 6, 2, 5, 3)
BATCH = ((0, 1), (2, 2), (4, 2), (6, 2), (1, 1))
PAIRS = NZ // 2
HP = 2 * HZ


def dot(a, b):
    return jnp.dot(a, b, preferred_element_type=F32)


def dot_t(a, b):
    return lax.dot_general(a, b, (((1,), (1,)), ((), ())), preferred_element_type=F32)


def wrap(v, n):
    return lax.rem(v + 2 * n, n)


def iota(shape, axis):
    return lax.broadcasted_iota(jnp.int32, shape, axis)


def kernel(
    emb, lists, owners, counts, item, cot, cd, cu, comp, of, w2, ot,
    out_hbm, eg_hbm,
    embv, listv, ownv, cntv, itemv, cotv, cdv, cuv, compv, ofv, W2, otv,
    hot, pay, arr, SR, lift, tsend, trecv, gsend, grecv, bpay, barr, egv,
    prei, hid, slope, pre2, g3, hs, gs2, outv, sacc,
    lsem, asend, arecv, tsem, trsem, gsem, grsem, bsend, brecv,
    zs, zr, ys, yr, xs, xr, ds, dr,
):
    t = lax.axis_index("tower")
    p = lax.axis_index("peer")
    x, c = t // NC, t % NC
    y, z = p % NY, p // NY
    px = x % 2
    c64 = c * 64

    def peer_at(dz, dy):
        return (t, wrap(z + dz, NZ) * NY + wrap(y + dy, NY))

    def far_first(i):
        a, b = i // NY, i % NY
        ka, kb = (a + 1) // 2, (b + 1) // 2
        dz = NZ // 2 + ka * (1 - 2 * (a % 2))
        dy = NY // 2 + kb * (1 - 2 * (b % 2))
        return dz, dy

    loads = [
        (emb, embv), (lists, listv), (w2, W2.at[0, y]), (owners, ownv), (counts, cntv), (item, itemv),
    ]
    for s in range(NZ):
        zz = wrap(z + ZREL[s], NZ)
        part = ofv.at[s // 2, :, pl.ds((s % 2) * HZ, HZ)]
        loads.append((of.at[:, pl.ds(pl.multiple_of(zz * HZ, HZ), HZ)], part))
    loads += [(cot, cotv), (ot, otv), (cd, cdv), (cu, cuv), (comp, compv)]
    copies = [pltpu.make_async_copy(a, b, lsem.at[i]) for i, (a, b) in enumerate(loads)]
    for cp in copies:
        cp.start()
    L_EMB, L_LIST, L_W2, L_OWN, L_CNT, L_ITEM, L_OF = 0, 1, 2, 3, 4, 5, 6
    L_COT, L_OT, L_CD, L_CU, L_COMP = 14, 15, 16, 17, 18

    barrier = pltpu.get_barrier_semaphore()

    def greet_peer(i, carry):
        dz, dy = far_first(i)
        pl.semaphore_signal(barrier, inc=1, device_id=peer_at(dz, dy), device_id_type=MESH)
        return carry

    lax.fori_loop(0, NP - 1, greet_peer, 0)

    def greet_tower(i, carry):
        pl.semaphore_signal(barrier, inc=1, device_id=(wrap(t + i, NT), p), device_id_type=MESH)
        return carry

    lax.fori_loop(1, NT, greet_tower, 0)

    copies[L_EMB].wait()
    copies[L_LIST].wait()
    order = listv[...]
    inner = order & (RBLK - 1)
    quarter = order >> 9
    lane = iota((32, 128), 1)

    def build_hot(k, carry):
        r0 = pl.multiple_of(k * 64, 64)
        rows = iota((64, LISTED), 0) + r0
        hot[pl.ds(r0, 64), :] = jnp.where(rows == inner, 1.0, 0.0).astype(BF16)
        return carry

    lax.fori_loop(0, RBLK // 64, build_hot, 0)
    stacked = jnp.concatenate([embv[:, k * RBLK:(k + 1) * RBLK] for k in range(FOLD)], axis=0)
    for n in range(4):
        cols = slice(n * 512, (n + 1) * 512)
        got = dot(stacked, hot[:, cols])
        q = quarter[:, cols]
        srt = jnp.where(q == 0, got[0:64], 0.0)
        for k in range(1, FOLD):
            srt = srt + jnp.where(q == k, got[k * 64:(k + 1) * 64], 0.0)
        for b in range(4):
            blk = srt[:, b * 128:(b + 1) * 128]
            both = jnp.concatenate([blk, pltpu.roll(blk, 96, 1)], axis=0)
            turned = both.T.astype(BF16)
            pay[n * 8 + b * 2] = turned[0:32]
            pay[n * 8 + b * 2 + 1] = turned[64:96]

    pl.semaphore_wait(barrier, NP - 1 + NT - 1)

    def exchange(src, dst, ssem, rsem):
        def one(i, carry):
            dz, dy = far_first(i)
            to = peer_at(dz, dy)
            pltpu.make_async_remote_copy(
                src_ref=src.at[to[1]], dst_ref=dst.at[p], send_sem=ssem, recv_sem=rsem,
                device_id=to, device_id_type=MESH,
            ).start()
            return carry

        lax.fori_loop(0, NP - 1, one, 0)
        dst[p] = src[p]

    def exchange_wait(dst, sem):
        part = dst.at[pl.ds(0, NP - 1)]
        pltpu.make_async_copy(part, part, sem).wait()

    def towers(src, dst, ssem, rsem):
        for i in range(1, NT):
            to = wrap(t + i, NT)
            pltpu.make_async_remote_copy(
                src_ref=src.at[pl.ds(pl.multiple_of(to * CAP, CAP), CAP)],
                dst_ref=dst.at[pl.ds(pl.multiple_of(t * CAP, CAP), CAP)],
                send_sem=ssem, recv_sem=rsem, device_id=(to, p), device_id_type=MESH,
            ).start()
        mine = pl.ds(pl.multiple_of(t * CAP, CAP), CAP)
        dst[mine] = src[mine]

    def towers_wait(dst, sem):
        part = dst.at[pl.ds(0, SLOTS - CAP)]
        pltpu.make_async_copy(part, part, sem).wait()

    ym, yp, yq = wrap(y - 1, NY), wrap(y + 1, NY), wrap(y + 2, NY)
    SETS = (ym, yp, yq, y)
    near = c64 + px * 32
    other = c64 + (1 - px) * 32
    sent = []

    def start(cp):
        cp.start()
        sent.append(cp)

    def rcopy(src, dst, ssem, rsem, to):
        return pltpu.make_async_remote_copy(
            src_ref=src, dst_ref=dst, send_sem=ssem, recv_sem=rsem, device_id=to, device_id_type=MESH
        )

    def rows(slot, r0, n):
        return W2.at[slot, y, pl.ds(pl.multiple_of(near + r0, 16), n)]

    def rows_b(b, k, r0, n):
        s0, m = BATCH[b]
        return W2.at[pl.ds(s0, m), SETS[k], pl.ds(pl.multiple_of(r0, 16), n)]

    def zc(i):
        a, b, r0, n, d = (
            (0, 2, 0, 32, 1), (0, 3, 0, 32, -1), (0, 4, 0, 32, 2), (0, 5, 0, 32, -2),
            (4, 6, 0, 32, 1), (5, 7, 0, 32, -1), (4, 1, 0, 16, 2), (5, 1, 16, 16, -2),
        )[i]
        return rcopy(rows(a, r0, n), rows(b, r0, n), zs.at[i], zr.at[i], peer_at(d, 0))

    def same(part, ssem, rsem, e, to):
        return rcopy(part, part, ssem.at[e], rsem.at[e], to)

    def y1(b):
        return [same(rows_b(b, 3, near, 32), ys, yr, b * 4 + i, peer_at(0, d)) for i, d in enumerate((1, -1))]

    def y2(b):
        return [same(rows_b(b, i, near + 16 * i, 16), ys, yr, b * 4 + 2 + i, peer_at(0, d)) for i, d in enumerate((1, -1))]

    def xc(b, k):
        return [
            same(rows_b(b, k, near + 16 * i, 16), xs, xr, b * 8 + k * 2 + i, (wrap(x + d, NX) * NC + c, p))
            for i, d in enumerate((1, -1))
        ]

    def dc(b, k, o):
        return same(rows_b(b, k, other if o else near, 32), ds, dr, b * 8 + k * 2 + o, (x * NC + 1 - c, p))

    def own(b):
        for cp in y1(b) + xc(b, 3):
            start(cp)
        start(dc(b, 3, 0))

    def ez(b):
        for i in ((), (0, 1), (2, 3), (4, 5), (6, 7))[b]:
            zc(i).wait_recv()
        if b == 2:
            for i in (4, 5, 6, 7):
                start(zc(i))
        own(b)

    def ey(b):
        for cp in y1(b):
            cp.wait_recv()
        for cp in y2(b) + xc(b, 0) + xc(b, 1):
            start(cp)
        for k in (0, 1):
            start(dc(b, k, 0))

    def ey2(b):
        for cp in y2(b):
            cp.wait_recv()
        for cp in xc(b, 2):
            start(cp)
        start(dc(b, 2, 0))

    def ex(b, *ks):
        for k in ks:
            for cp in xc(b, k):
                cp.wait_recv()
            start(dc(b, k, 1))

    def ed(b):
        for k in range(4 if b else 3):
            for o in (0, 1):
                dc(b, k, o).wait_recv()

    copies[L_W2].wait()
    for i in (0, 1):
        start(zc(i))
    for cp in y1(0):
        start(cp)
    for i in (2, 3):
        start(zc(i))
    exchange(pay, arr, asend, arecv)

    copies[L_ITEM].wait()
    for s in range(NZ):
        copies[L_OF + s].wait()

    def item_step(q, carry):
        for h in (slice(0, HZ), slice(HZ, HP)):
            prei[q, :, h] = dot(itemv[...], ofv[q, WIDE:, h])
        return carry

    lax.fori_loop(0, PAIRS // 2, item_step, 0)
    ez(1)
    ey(0)
    lax.fori_loop(PAIRS // 2, PAIRS, item_step, 0)
    ez(2)
    ey2(0)
    ey(1)
    copies[L_COT].wait()
    copies[L_OT].wait()

    def cot_step(n, carry):
        r0 = pl.multiple_of(n * 512, 512)
        g3[:, pl.ds(r0, 512)] = dot_t(cotv[...], otv[pl.ds(r0, 512), :])
        return carry

    lax.fori_loop(0, 2, cot_step, 0)
    ez(3)
    ez(4)
    ey(2)
    ex(1, 3)
    ex(0, 0, 1)

    copies[L_OWN].wait()
    copies[L_CNT].wait()
    own = ownv[...]
    choose = jnp.where(iota((8, UDEV), 0) == own, 1.0, 0.0)
    before = jnp.where(iota((UDEV, UDEV), 0) < iota((UDEV, UDEV), 1), 1.0, 0.0).astype(BF16)
    earlier = dot(choose.astype(BF16), before)
    pos = jnp.sum(choose * earlier, axis=0, keepdims=True)
    target = own * CAP + pos.astype(jnp.int32)
    hit = iota((SLOTS, UDEV), 0) == target
    disp = jnp.where(hit, 1.0, 0.0).astype(BF16)
    held = dot(jnp.where(hit, cntv[...].astype(F32), 0.0).astype(BF16), jnp.ones((UDEV, 128), BF16))
    tsend[:, WIDE:] = held.astype(BF16)
    for i in (L_CD, L_CU, L_COMP):
        copies[i].wait()

    exchange_wait(arr, arecv)

    def lay(j, carry):
        a = arr[2 * j].astype(F32)
        b = arr[2 * j + 1].astype(F32)
        at = pl.ds(pl.multiple_of(j * 128, 128), 128)
        SR[0:32, at] = jnp.where(lane < 64, a, pltpu.roll(b, 64, 1)).astype(BF16)
        SR[32:64, at] = jnp.where(lane < 64, pltpu.roll(a, 64, 1), b).astype(BF16)
        return carry

    lax.fori_loop(0, NP // 2, lay, 0)
    low = dot(SR[...], cdv[...]).astype(BF16)
    lift[...] = dot(low, cuv[...])
    wide = SR[...].astype(F32)
    crossed = (wide * lift[...] + wide).astype(BF16)
    compressed = dot(crossed, compv[...]).astype(BF16)
    tsend[:, :WIDE] = dot(disp, compressed).astype(BF16)
    towers(tsend, trecv, tsem, trsem)

    ey2(1)
    ex(2, 3)
    ex(0, 2)
    ey(3)
    ey(4)
    ey2(2)
    ex(1, 0, 1)
    ey2(3)
    ey2(4)
    ex(3, 3)
    ex(4, 3)

    towers_wait(trecv, trsem)
    qi = iota((ROWS, SLOTS), 0)
    si = iota((ROWS, SLOTS), 1) * MOSTC
    spread = jnp.where((qi >= si) & (qi < si + MOSTC), 1.0, 0.0).astype(BF16)
    grid = dot(spread, trecv[...])
    expanded = grid[:, :WIDE].astype(BF16)
    third = (qi * 21846) >> 16
    live = jnp.where((qi - third * MOSTC).astype(F32) < grid[:, WIDE:], 1.0, 0.0)[:, 0:1]

    def first_step(q, carry):
        for h in (slice(0, HZ), slice(HZ, HP)):
            pre = prei[q, :, h] + dot(expanded, ofv[q, :WIDE, h])
            sig = 0.5 * jnp.tanh(0.5 * pre) + 0.5
            act = pre * sig
            hid[q, :, h] = act.astype(BF16)
            slope[q, :, h] = (sig + act * (1.0 - sig)).astype(BF16)
        return carry

    def pair(q):
        return W2[pl.ds(2 * q, 2)].reshape(HP, H2)

    lax.fori_loop(0, PAIRS // 2, first_step, 0)
    ex(1, 2)
    ex(2, 0, 1)
    ex(2, 2)
    lax.fori_loop(PAIRS // 2, PAIRS, first_step, 0)
    ex(3, 0, 1)
    ex(4, 0, 1)
    ed(1)
    pre2[...] = dot(hid[1], pair(1))
    ex(3, 2)
    ex(4, 2)
    ed(2)
    pre2[...] += dot(hid[2], pair(2))
    ed(3)
    pre2[...] += dot(hid[3], pair(3))
    ed(0)
    ed(4)
    pre2[...] += dot(hid[0], pair(0))

    def mid_step(n, carry):
        at = pl.ds(pl.multiple_of(n * 256, 256), 256)
        pre = pre2[:, at]
        sig = 0.5 * jnp.tanh(0.5 * pre) + 0.5
        act = pre * sig
        hs[:, at] = act.astype(BF16)
        gs2[:, at] = (g3[:, at] * live * (sig + act * (1.0 - sig))).astype(BF16)
        return carry

    lax.fori_loop(0, 4, mid_step, 0)
    sacc[...] = jnp.zeros_like(sacc)

    def back_step(q, carry):
        g = (dot_t(gs2[...], pair(q)) * slope[q].astype(F32)).astype(BF16)
        sacc[...] += dot_t(g, ofv[q, :WIDE, :])
        return carry

    lax.fori_loop(0, PAIRS, back_step, 0)
    qj = iota((SLOTS, ROWS), 1)
    sj = iota((SLOTS, ROWS), 0) * MOSTC
    gather3 = jnp.where((qj >= sj) & (qj < sj + MOSTC), 1.0, 0.0).astype(BF16)
    gsend[...] = dot(gather3, sacc[...].astype(BF16)).astype(BF16)
    towers(gsend, grecv, gsem, grsem)

    def out_step(n, carry):
        at = pl.ds(pl.multiple_of(n * 256, 256), 256)
        outv[:, at] = (dot(hs[...], otv[:, at]) * live).astype(BF16)
        return carry

    lax.fori_loop(0, 4, out_step, 0)
    out_copy = pltpu.make_async_copy(outv, out_hbm, lsem.at[19])
    out_copy.start()

    towers_wait(grecv, grsem)
    eye = jnp.where(iota((UDEV, UDEV), 0) == iota((UDEV, UDEV), 1), 1.0, 0.0).astype(BF16)
    undisp = dot_t(eye, disp).astype(BF16)
    session_grad = dot(undisp, grecv[...]).astype(BF16)
    gc = dot_t(session_grad, compv[...]).astype(BF16).astype(F32)
    gl = (gc * SR[...].astype(F32)).astype(BF16)
    glow = dot_t(gl, cuv[...]).astype(BF16)
    lift[...] = gc * (lift[...] + 1.0) + dot_t(glow, cdv[...])

    def unlay(j, carry):
        at = pl.ds(pl.multiple_of(j * 128, 128), 128)
        lo = lift[0:32, at]
        hi = lift[32:64, at]
        bpay[2 * j] = jnp.where(lane < 64, lo, pltpu.roll(hi, 64, 1)).astype(BF16)
        bpay[2 * j + 1] = jnp.where(lane < 64, pltpu.roll(lo, 64, 1), hi).astype(BF16)
        return carry

    lax.fori_loop(0, NP // 2, unlay, 0)
    exchange(bpay, barr, bsend, brecv)
    for cp in sent:
        cp.wait_send()
    exchange_wait(pay, asend)
    towers_wait(tsend, tsem)
    towers_wait(gsend, gsem)
    exchange_wait(barr, brecv)

    total = jnp.zeros((FOLD * 64, RBLK), F32)
    zero = jnp.zeros((32, 128), F32)
    lane64 = iota((64, 128), 1) & 63
    for n in range(4):
        parts = []
        for b in range(4):
            p0 = n * 8 + b * 2
            tall = jnp.concatenate([barr[p0].astype(F32), zero, barr[p0 + 1].astype(F32), zero], axis=0)
            turned = tall.T
            parts.append(jnp.where(lane64 < 32, turned[0:64], pltpu.roll(turned[64:128], 32, 1)))
        grads = jnp.concatenate(parts, axis=1)
        q = quarter[:, n * 512:(n + 1) * 512]
        laid = jnp.concatenate([jnp.where(q == k, grads, 0.0).astype(BF16) for k in range(FOLD)], axis=0)
        total = total + dot_t(laid, hot[:, n * 512:(n + 1) * 512])
    for k in range(FOLD):
        egv[:, k * RBLK:(k + 1) * RBLK] = total[k * 64:(k + 1) * 64].astype(BF16)
    eg_copy = pltpu.make_async_copy(egv, eg_hbm, lsem.at[20])
    eg_copy.start()
    exchange_wait(bpay, bsend)
    out_copy.wait()
    eg_copy.wait()


def body(
    embeddings, session_lists, owners, counts, item_feats, cotangent,
    cross_down, cross_up, compress, over_first, over_second, over_third,
):
    dma = pltpu.SemaphoreType.DMA
    vm = pltpu.VMEM
    scratch = [
        vm((64, LISTED), BF16), vm((1, LISTED), jnp.int32), vm((1, UDEV), jnp.int32), vm((1, UDEV), jnp.int32),
        vm((ROWS, WIDE), BF16), vm((ROWS, H2), BF16), vm((FEAT, WIDE), BF16), vm((WIDE, FEAT), BF16),
        vm((FEAT, WIDE), BF16), vm((PAIRS, 2 * WIDE, HP), BF16), vm((NZ, NY, HS, H2), BF16), vm((H2, H2), BF16),
        vm((RBLK, LISTED), BF16), vm((NP, 32, 128), BF16), vm((NP, 32, 128), BF16), vm((UDEV, FEAT), BF16),
        vm((UDEV, FEAT), F32), vm((SLOTS, WIDE + 128), BF16), vm((SLOTS, WIDE + 128), BF16),
        vm((SLOTS, WIDE), BF16), vm((SLOTS, WIDE), BF16), vm((NP, 32, 128), BF16), vm((NP, 32, 128), BF16),
        vm((64, LISTED), BF16),
        vm((PAIRS, ROWS, HP), F32), vm((PAIRS, ROWS, HP), BF16), vm((PAIRS, ROWS, HP), BF16), vm((ROWS, H2), F32),
        vm((ROWS, H2), F32), vm((ROWS, H2), BF16), vm((ROWS, H2), BF16), vm((ROWS, H2), BF16), vm((ROWS, WIDE), F32),
        dma((21,)), dma, dma, dma, dma, dma, dma, dma, dma,
        dma((8,)), dma((8,)), dma((20,)), dma((20,)), dma((40,)), dma((40,)), dma((40,)), dma((40,)),
    ]
    anywhere = pl.BlockSpec(memory_space=pl.ANY)
    over_out, emb_grad_t = pl.pallas_call(
        kernel,
        out_shape=(
            jax.ShapeDtypeStruct((ROWS, H2), BF16),
            jax.ShapeDtypeStruct((64, LISTED), BF16),
        ),
        in_specs=[anywhere] * 12,
        out_specs=(anywhere, anywhere),
        scratch_shapes=scratch,
        compiler_params=pltpu.CompilerParams(
            collective_id=0, has_side_effects=True, vmem_limit_bytes=60 * 2**20
        ),
    )(
        embeddings.T, session_lists, owners.reshape(1, UDEV), counts.reshape(1, UDEV), item_feats, cotangent,
        cross_down, cross_up, compress, over_first, over_second, over_third,
    )
    return over_out, emb_grad_t.T


def solution(mesh):
    return jax.shard_map(
        body,
        mesh=mesh,
        in_specs=(
            P("tower", "peer"),
            P("tower", None),
            P(("tower", "peer"), None),
            P(("tower", "peer")),
            P(("tower", "peer"), None),
            P(("tower", "peer"), None),
            P(),
            P(),
            P(),
            P(),
            P("peer", None),
            P(),
        ),
        out_specs=(P(("tower", "peer"), None), P("tower", "peer")),
        check_vma=False,
    )
```

```python
import jax
import jax.numpy as jnp
from jax import lax
from jax.experimental import pallas as pl
from jax.experimental.pallas import tpu as pltpu
from jax.sharding import PartitionSpec as P

MESH = pl.DeviceIdType.MESH
F32 = jnp.float32
BF16 = jnp.bfloat16
NX, NC, NY, NZ = 4, 2, 4, 8
NP, NT = NY * NZ, NX * NC
ROWS, SLOTS, MOSTC, CAP = 384, 128, 3, 16
UDEV = 64
FEAT, WIDE = 2048, 256
H1, H2 = 4096, 1024
HZ = H1 // NZ
HS = H1 // NP
LISTED = UDEV * NP
FOLD = 4
RBLK = LISTED // FOLD
ZREL = (0, 4, 7, 1, 6, 2, 5, 3)
BATCH = ((0, 1), (2, 2), (4, 2), (6, 2), (1, 1))
PAIRS = NZ // 2
HP = 2 * HZ


def dot(a, b):
    return jnp.dot(a, b, preferred_element_type=F32)


def dot_t(a, b):
    return lax.dot_general(a, b, (((1,), (1,)), ((), ())), preferred_element_type=F32)


def wrap(v, n):
    return lax.rem(v + 2 * n, n)


def iota(shape, axis):
    return lax.broadcasted_iota(jnp.int32, shape, axis)


def kernel(
    emb, lists, owners, counts, item, cot, cd, cu, comp, of, w2, ot,
    out_hbm, eg_hbm,
    embv, listv, ownv, cntv, itemv, cotv, cdv, cuv, compv, ofv, W2, otv,
    hot, pay, arr, SR, lift, tsend, trecv, gsend, grecv, bpay, barr, egv,
    prei, hid, slope, pre2, g3, hs, gs2, outv, sacc,
    lsem, asend, arecv, tsem, trsem, gsem, grsem, bsend, brecv,
    zs, zr, ys, yr, xs, xr, ds, dr, hop1, hop2,
):
    t = lax.axis_index("tower")
    p = lax.axis_index("peer")
    x, c = t // NC, t % NC
    y, z = p % NY, p // NY
    px = x % 2
    c64 = c * 64

    def peer_at(dz, dy):
        return (t, wrap(z + dz, NZ) * NY + wrap(y + dy, NY))

    def far_first(i):
        a, b = i // NY, i % NY
        ka, kb = (a + 1) // 2, (b + 1) // 2
        dz = NZ // 2 + ka * (1 - 2 * (a % 2))
        dy = NY // 2 + kb * (1 - 2 * (b % 2))
        return dz, dy

    barrier = pltpu.get_barrier_semaphore()

    close = tuple(peer_at(d, 0) for d in (-1, 1, -2, 2))
    for to in close + tuple(peer_at(0, d) for d in (-1, 1, 2)):
        pl.semaphore_signal(barrier, inc=1, device_id=to, device_id_type=MESH)

    def greet_tower(i, carry):
        pl.semaphore_signal(barrier, inc=1, device_id=(wrap(t + i, NT), p), device_id_type=MESH)
        return carry

    lax.fori_loop(1, NT, greet_tower, 0)

    loads = [
        (w2, W2.at[0, y]), (emb, embv), (lists, listv), (owners, ownv), (counts, cntv), (item, itemv),
    ]
    for s in range(NZ):
        zz = wrap(z + ZREL[s], NZ)
        part = ofv.at[s // 2, :, pl.ds((s % 2) * HZ, HZ)]
        loads.append((of.at[:, pl.ds(pl.multiple_of(zz * HZ, HZ), HZ)], part))
    loads += [(cot, cotv), (ot, otv), (cd, cdv), (cu, cuv), (comp, compv)]
    copies = [pltpu.make_async_copy(a, b, lsem.at[i]) for i, (a, b) in enumerate(loads)]
    for cp in copies:
        cp.start()
    L_W2, L_EMB, L_LIST, L_OWN, L_CNT, L_ITEM, L_OF = 0, 1, 2, 3, 4, 5, 6
    L_COT, L_OT, L_CD, L_CU, L_COMP = 14, 15, 16, 17, 18

    def exchange(src, dst, ssem, rsem):
        def one(i, carry):
            dz, dy = far_first(i)
            to = peer_at(dz, dy)
            pltpu.make_async_remote_copy(
                src_ref=src.at[to[1]], dst_ref=dst.at[p], send_sem=ssem, recv_sem=rsem,
                device_id=to, device_id_type=MESH,
            ).start()
            return carry

        lax.fori_loop(0, NP - 1, one, 0)
        dst[p] = src[p]

    def exchange_wait(dst, sem):
        part = dst.at[pl.ds(0, NP - 1)]
        pltpu.make_async_copy(part, part, sem).wait()

    def towers(src, dst, ssem, rsem):
        for i in range(1, NT):
            to = wrap(t + i, NT)
            pltpu.make_async_remote_copy(
                src_ref=src.at[pl.ds(pl.multiple_of(to * CAP, CAP), CAP)],
                dst_ref=dst.at[pl.ds(pl.multiple_of(t * CAP, CAP), CAP)],
                send_sem=ssem, recv_sem=rsem, device_id=(to, p), device_id_type=MESH,
            ).start()
        mine = pl.ds(pl.multiple_of(t * CAP, CAP), CAP)
        dst[mine] = src[mine]

    def towers_wait(dst, sem):
        part = dst.at[pl.ds(0, SLOTS - CAP)]
        pltpu.make_async_copy(part, part, sem).wait()

    ym, yp, yq = wrap(y - 1, NY), wrap(y + 1, NY), wrap(y + 2, NY)
    SETS = (ym, yp, yq, y)
    near = c64 + px * 32
    other = c64 + (1 - px) * 32
    sent = []

    def start(cp):
        cp.start()
        sent.append(cp)

    def rcopy(src, dst, ssem, rsem, to):
        return pltpu.make_async_remote_copy(
            src_ref=src, dst_ref=dst, send_sem=ssem, recv_sem=rsem, device_id=to, device_id_type=MESH
        )

    def rows(slot, r0, n):
        return W2.at[slot, y, pl.ds(pl.multiple_of(near + r0, 16), n)]

    def rows_b(b, k, r0, n):
        s0, m = BATCH[b]
        return W2.at[pl.ds(s0, m), SETS[k], pl.ds(pl.multiple_of(r0, 16), n)]

    def zc(i):
        a, b, r0, n, d = (
            (0, 2, 0, 32, 1), (0, 3, 0, 32, -1), (0, 4, 0, 32, 2), (0, 5, 0, 32, -2),
            (4, 6, 0, 32, 1), (5, 7, 0, 32, -1), (4, 1, 0, 16, 2), (5, 1, 16, 16, -2),
        )[i]
        return rcopy(rows(a, r0, n), rows(b, r0, n), zs.at[i], zr.at[i], peer_at(d, 0))

    def same(part, ssem, rsem, e, to):
        return rcopy(part, part, ssem.at[e], rsem.at[e], to)

    def y1(b):
        return [same(rows_b(b, 3, near, 32), ys, yr, b * 4 + i, peer_at(0, d)) for i, d in enumerate((1, -1))]

    def y2(b):
        return [same(rows_b(b, i, near + 16 * i, 16), ys, yr, b * 4 + 2 + i, peer_at(0, d)) for i, d in enumerate((1, -1))]

    def xc(b, k):
        return [
            same(rows_b(b, k, near + 16 * i, 16), xs, xr, b * 8 + k * 2 + i, (wrap(x + d, NX) * NC + c, p))
            for i, d in enumerate((1, -1))
        ]

    def dc(b, k, o):
        return same(rows_b(b, k, other if o else near, 32), ds, dr, b * 8 + k * 2 + o, (x * NC + 1 - c, p))

    def own(b):
        for cp in y1(b) + xc(b, 3):
            start(cp)
        start(dc(b, 3, 0))

    def ez(b):
        for i in ((), (0, 1), (2, 3), (4, 5), (6, 7))[b]:
            zc(i).wait_recv()
        if b == 2:
            for i in (4, 5, 6, 7):
                start(zc(i))
        own(b)

    def ey(b):
        for cp in y1(b):
            cp.wait_recv()
        for cp in y2(b) + xc(b, 0) + xc(b, 1):
            start(cp)
        for k in (0, 1):
            start(dc(b, k, 0))

    def ey2(b):
        for cp in y2(b):
            cp.wait_recv()
        for cp in xc(b, 2):
            start(cp)
        start(dc(b, 2, 0))

    def ex(b, *ks):
        for k in ks:
            for cp in xc(b, k):
                cp.wait_recv()
            start(dc(b, k, 1))

    def ed(b):
        for k in range(4 if b else 3):
            for o in (0, 1):
                dc(b, k, o).wait_recv()

    pl.semaphore_wait(barrier, NT - 1 + 7)
    for to in close:
        pl.semaphore_signal(hop1, inc=1, device_id=to, device_id_type=MESH)
    copies[L_W2].wait()
    for i in (0, 1):
        start(zc(i))
    for cp in y1(0):
        start(cp)
    for i in (2, 3):
        start(zc(i))

    copies[L_EMB].wait()
    copies[L_LIST].wait()
    order = listv[...]
    inner = order & (RBLK - 1)
    quarter = order >> 9
    lane = iota((32, 128), 1)

    def build_hot(k, carry):
        r0 = pl.multiple_of(k * 64, 64)
        rows = iota((64, LISTED), 0) + r0
        hot[pl.ds(r0, 64), :] = jnp.where(rows == inner, 1.0, 0.0).astype(BF16)
        return carry

    lax.fori_loop(0, RBLK // 64, build_hot, 0)
    stacked = jnp.concatenate([embv[:, k * RBLK:(k + 1) * RBLK] for k in range(FOLD)], axis=0)
    for n in range(4):
        cols = slice(n * 512, (n + 1) * 512)
        got = dot(stacked, hot[:, cols])
        q = quarter[:, cols]
        srt = jnp.where(q == 0, got[0:64], 0.0)
        for k in range(1, FOLD):
            srt = srt + jnp.where(q == k, got[k * 64:(k + 1) * 64], 0.0)
        for b in range(4):
            blk = srt[:, b * 128:(b + 1) * 128]
            both = jnp.concatenate([blk, pltpu.roll(blk, 96, 1)], axis=0)
            turned = both.T.astype(BF16)
            pay[n * 8 + b * 2] = turned[0:32]
            pay[n * 8 + b * 2 + 1] = turned[64:96]

    pl.semaphore_wait(hop1, 4)
    for to in close[2:]:
        pl.semaphore_signal(hop2, inc=1, device_id=to, device_id_type=MESH)

    copies[L_ITEM].wait()
    for s in range(NZ):
        copies[L_OF + s].wait()

    def item_step(q, carry):
        for h in (slice(0, HZ), slice(HZ, HP)):
            prei[q, :, h] = dot(itemv[...], ofv[q, WIDE:, h])
        return carry

    lax.fori_loop(0, PAIRS // 2, item_step, 0)
    ez(1)
    ey(0)
    lax.fori_loop(PAIRS // 2, PAIRS, item_step, 0)
    ez(2)
    pl.semaphore_wait(hop2, 2)
    exchange(pay, arr, asend, arecv)
    ey2(0)
    ey(1)
    copies[L_COT].wait()
    copies[L_OT].wait()

    def cot_step(n, carry):
        r0 = pl.multiple_of(n * 512, 512)
        g3[:, pl.ds(r0, 512)] = dot_t(cotv[...], otv[pl.ds(r0, 512), :])
        return carry

    lax.fori_loop(0, 2, cot_step, 0)
    ez(3)
    ez(4)
    ey(2)
    ex(1, 3)
    ex(0, 0, 1)

    copies[L_OWN].wait()
    copies[L_CNT].wait()
    own = ownv[...]
    choose = jnp.where(iota((8, UDEV), 0) == own, 1.0, 0.0)
    before = jnp.where(iota((UDEV, UDEV), 0) < iota((UDEV, UDEV), 1), 1.0, 0.0).astype(BF16)
    earlier = dot(choose.astype(BF16), before)
    pos = jnp.sum(choose * earlier, axis=0, keepdims=True)
    target = own * CAP + pos.astype(jnp.int32)
    hit = iota((SLOTS, UDEV), 0) == target
    disp = jnp.where(hit, 1.0, 0.0).astype(BF16)
    held = dot(jnp.where(hit, cntv[...].astype(F32), 0.0).astype(BF16), jnp.ones((UDEV, 128), BF16))
    tsend[:, WIDE:] = held.astype(BF16)
    for i in (L_CD, L_CU, L_COMP):
        copies[i].wait()

    exchange_wait(arr, arecv)

    def lay(j, carry):
        a = arr[2 * j].astype(F32)
        b = arr[2 * j + 1].astype(F32)
        at = pl.ds(pl.multiple_of(j * 128, 128), 128)
        SR[0:32, at] = jnp.where(lane < 64, a, pltpu.roll(b, 64, 1)).astype(BF16)
        SR[32:64, at] = jnp.where(lane < 64, pltpu.roll(a, 64, 1), b).astype(BF16)
        return carry

    lax.fori_loop(0, NP // 2, lay, 0)
    low = dot(SR[...], cdv[...]).astype(BF16)
    lift[...] = dot(low, cuv[...])
    wide = SR[...].astype(F32)
    crossed = (wide * lift[...] + wide).astype(BF16)
    compressed = dot(crossed, compv[...]).astype(BF16)
    tsend[:, :WIDE] = dot(disp, compressed).astype(BF16)
    towers(tsend, trecv, tsem, trsem)

    ey2(1)
    ex(2, 3)
    ex(0, 2)
    ey(3)
    ey(4)
    ey2(2)
    ex(1, 0, 1)
    ey2(3)
    ey2(4)
    ex(3, 3)
    ex(4, 3)

    towers_wait(trecv, trsem)
    qi = iota((ROWS, SLOTS), 0)
    si = iota((ROWS, SLOTS), 1) * MOSTC
    spread = jnp.where((qi >= si) & (qi < si + MOSTC), 1.0, 0.0).astype(BF16)
    grid = dot(spread, trecv[...])
    expanded = grid[:, :WIDE].astype(BF16)
    third = (qi * 21846) >> 16
    live = jnp.where((qi - third * MOSTC).astype(F32) < grid[:, WIDE:], 1.0, 0.0)[:, 0:1]

    def first_step(q, carry):
        for h in (slice(0, HZ), slice(HZ, HP)):
            pre = prei[q, :, h] + dot(expanded, ofv[q, :WIDE, h])
            sig = 0.5 * jnp.tanh(0.5 * pre) + 0.5
            act = pre * sig
            hid[q, :, h] = act.astype(BF16)
            slope[q, :, h] = (sig + act * (1.0 - sig)).astype(BF16)
        return carry

    def pair(q):
        return W2[pl.ds(2 * q, 2)].reshape(HP, H2)

    lax.fori_loop(0, PAIRS // 2, first_step, 0)
    ex(1, 2)
    ex(2, 0, 1)
    ex(2, 2)
    lax.fori_loop(PAIRS // 2, PAIRS, first_step, 0)
    ex(3, 0, 1)
    ex(4, 0, 1)
    ed(1)
    pre2[...] = dot(hid[1], pair(1))
    ex(3, 2)
    ex(4, 2)
    ed(2)
    pre2[...] += dot(hid[2], pair(2))
    ed(3)
    pre2[...] += dot(hid[3], pair(3))
    ed(0)
    ed(4)
    pre2[...] += dot(hid[0], pair(0))

    def mid_step(n, carry):
        at = pl.ds(pl.multiple_of(n * 256, 256), 256)
        pre = pre2[:, at]
        sig = 0.5 * jnp.tanh(0.5 * pre) + 0.5
        act = pre * sig
        hs[:, at] = act.astype(BF16)
        gs2[:, at] = (g3[:, at] * live * (sig + act * (1.0 - sig))).astype(BF16)
        return carry

    lax.fori_loop(0, 4, mid_step, 0)
    sacc[...] = jnp.zeros_like(sacc)

    def back_step(q, carry):
        g = (dot_t(gs2[...], pair(q)) * slope[q].astype(F32)).astype(BF16)
        sacc[...] += dot_t(g, ofv[q, :WIDE, :])
        return carry

    lax.fori_loop(0, PAIRS, back_step, 0)
    qj = iota((SLOTS, ROWS), 1)
    sj = iota((SLOTS, ROWS), 0) * MOSTC
    gather3 = jnp.where((qj >= sj) & (qj < sj + MOSTC), 1.0, 0.0).astype(BF16)
    gsend[...] = dot(gather3, sacc[...].astype(BF16)).astype(BF16)
    towers(gsend, grecv, gsem, grsem)

    def out_step(n, carry):
        at = pl.ds(pl.multiple_of(n * 256, 256), 256)
        outv[:, at] = (dot(hs[...], otv[:, at]) * live).astype(BF16)
        return carry

    lax.fori_loop(0, 4, out_step, 0)
    out_copy = pltpu.make_async_copy(outv, out_hbm, lsem.at[19])
    out_copy.start()

    towers_wait(grecv, grsem)
    eye = jnp.where(iota((UDEV, UDEV), 0) == iota((UDEV, UDEV), 1), 1.0, 0.0).astype(BF16)
    undisp = dot_t(eye, disp).astype(BF16)
    session_grad = dot(undisp, grecv[...]).astype(BF16)
    gc = dot_t(session_grad, compv[...]).astype(BF16).astype(F32)
    gl = (gc * SR[...].astype(F32)).astype(BF16)
    glow = dot_t(gl, cuv[...]).astype(BF16)
    lift[...] = gc * (lift[...] + 1.0) + dot_t(glow, cdv[...])

    def unlay(j, carry):
        at = pl.ds(pl.multiple_of(j * 128, 128), 128)
        lo = lift[0:32, at]
        hi = lift[32:64, at]
        bpay[2 * j] = jnp.where(lane < 64, lo, pltpu.roll(hi, 64, 1)).astype(BF16)
        bpay[2 * j + 1] = jnp.where(lane < 64, pltpu.roll(lo, 64, 1), hi).astype(BF16)
        return carry

    lax.fori_loop(0, NP // 2, unlay, 0)
    exchange(bpay, barr, bsend, brecv)
    for cp in sent:
        cp.wait_send()
    exchange_wait(pay, asend)
    towers_wait(tsend, tsem)
    towers_wait(gsend, gsem)
    exchange_wait(barr, brecv)

    total = jnp.zeros((FOLD * 64, RBLK), F32)
    zero = jnp.zeros((32, 128), F32)
    lane64 = iota((64, 128), 1) & 63
    for n in range(4):
        parts = []
        for b in range(4):
            p0 = n * 8 + b * 2
            tall = jnp.concatenate([barr[p0].astype(F32), zero, barr[p0 + 1].astype(F32), zero], axis=0)
            turned = tall.T
            parts.append(jnp.where(lane64 < 32, turned[0:64], pltpu.roll(turned[64:128], 32, 1)))
        grads = jnp.concatenate(parts, axis=1)
        q = quarter[:, n * 512:(n + 1) * 512]
        laid = jnp.concatenate([jnp.where(q == k, grads, 0.0).astype(BF16) for k in range(FOLD)], axis=0)
        total = total + dot_t(laid, hot[:, n * 512:(n + 1) * 512])
    for k in range(FOLD):
        egv[:, k * RBLK:(k + 1) * RBLK] = total[k * 64:(k + 1) * 64].astype(BF16)
    eg_copy = pltpu.make_async_copy(egv, eg_hbm, lsem.at[20])
    eg_copy.start()
    exchange_wait(bpay, bsend)
    out_copy.wait()
    eg_copy.wait()


def body(
    embeddings, session_lists, owners, counts, item_feats, cotangent,
    cross_down, cross_up, compress, over_first, over_second, over_third,
):
    dma = pltpu.SemaphoreType.DMA
    vm = pltpu.VMEM
    scratch = [
        vm((64, LISTED), BF16), vm((1, LISTED), jnp.int32), vm((1, UDEV), jnp.int32), vm((1, UDEV), jnp.int32),
        vm((ROWS, WIDE), BF16), vm((ROWS, H2), BF16), vm((FEAT, WIDE), BF16), vm((WIDE, FEAT), BF16),
        vm((FEAT, WIDE), BF16), vm((PAIRS, 2 * WIDE, HP), BF16), vm((NZ, NY, HS, H2), BF16), vm((H2, H2), BF16),
        vm((RBLK, LISTED), BF16), vm((NP, 32, 128), BF16), vm((NP, 32, 128), BF16), vm((UDEV, FEAT), BF16),
        vm((UDEV, FEAT), F32), vm((SLOTS, WIDE + 128), BF16), vm((SLOTS, WIDE + 128), BF16),
        vm((SLOTS, WIDE), BF16), vm((SLOTS, WIDE), BF16), vm((NP, 32, 128), BF16), vm((NP, 32, 128), BF16),
        vm((64, LISTED), BF16),
        vm((PAIRS, ROWS, HP), F32), vm((PAIRS, ROWS, HP), BF16), vm((PAIRS, ROWS, HP), BF16), vm((ROWS, H2), F32),
        vm((ROWS, H2), F32), vm((ROWS, H2), BF16), vm((ROWS, H2), BF16), vm((ROWS, H2), BF16), vm((ROWS, WIDE), F32),
        dma((21,)), dma, dma, dma, dma, dma, dma, dma, dma,
        dma((8,)), dma((8,)), dma((20,)), dma((20,)), dma((40,)), dma((40,)), dma((40,)), dma((40,)),
        pltpu.SemaphoreType.REGULAR, pltpu.SemaphoreType.REGULAR,
    ]
    anywhere = pl.BlockSpec(memory_space=pl.ANY)
    over_out, emb_grad_t = pl.pallas_call(
        kernel,
        out_shape=(
            jax.ShapeDtypeStruct((ROWS, H2), BF16),
            jax.ShapeDtypeStruct((64, LISTED), BF16),
        ),
        in_specs=[anywhere] * 12,
        out_specs=(anywhere, anywhere),
        scratch_shapes=scratch,
        compiler_params=pltpu.CompilerParams(
            collective_id=0, has_side_effects=True, vmem_limit_bytes=60 * 2**20
        ),
    )(
        embeddings.T, session_lists, owners.reshape(1, UDEV), counts.reshape(1, UDEV), item_feats, cotangent,
        cross_down, cross_up, compress, over_first, over_second, over_third,
    )
    return over_out, emb_grad_t.T


def solution(mesh):
    return jax.shard_map(
        body,
        mesh=mesh,
        in_specs=(
            P("tower", "peer"),
            P("tower", None),
            P(("tower", "peer"), None),
            P(("tower", "peer")),
            P(("tower", "peer"), None),
            P(("tower", "peer"), None),
            P(),
            P(),
            P(),
            P(),
            P("peer", None),
            P(),
        ),
        out_specs=(P(("tower", "peer"), None), P("tower", "peer")),
        check_vma=False,
    )
```

```python
import jax
import jax.numpy as jnp
from jax import lax
from jax.experimental import pallas as pl
from jax.experimental.pallas import tpu as pltpu
from jax.sharding import PartitionSpec as P

MESH = pl.DeviceIdType.MESH
F32 = jnp.float32
BF16 = jnp.bfloat16
NX, NC, NY, NZ = 4, 2, 4, 8
NP, NT = NY * NZ, NX * NC
ROWS, SLOTS, MOSTC, CAP = 384, 128, 3, 16
UDEV = 64
FEAT, WIDE = 2048, 256
H1, H2 = 4096, 1024
HZ = H1 // NZ
HS = H1 // NP
LISTED = UDEV * NP
FOLD = 4
RBLK = LISTED // FOLD
ZREL = (0, 4, 7, 1, 6, 2, 5, 3)
BATCH = ((0, 1), (2, 2), (4, 2), (6, 2), (1, 1))
PAIRS = NZ // 2
HP = 2 * HZ


def dot(a, b):
    return jnp.dot(a, b, preferred_element_type=F32)


def dot_t(a, b):
    return lax.dot_general(a, b, (((1,), (1,)), ((), ())), preferred_element_type=F32)


def wrap(v, n):
    return lax.rem(v + 2 * n, n)


def iota(shape, axis):
    return lax.broadcasted_iota(jnp.int32, shape, axis)


def kernel(
    emb, lists, owners, counts, item, cot, cd, cu, comp, of, w2, ot,
    out_hbm, eg_hbm,
    embv, listv, ownv, cntv, itemv, cotv, cdv, cuv, compv, ofv, W2, otv,
    hot, pay, arr, SR, lift, tsend, trecv, gsend, grecv, bpay, barr, egv,
    prei, hid, slope, pre2, g3, hs, gs2, outv, cdT, cuT, compT, gcv,
    lsem, asend, arecv, tsem, trsem, gsem, grsem, bsend, brecv,
    zs, zr, ys, yr, xs, xr, ds, dr, hop1, hop2,
):
    t = lax.axis_index("tower")
    p = lax.axis_index("peer")
    x, c = t // NC, t % NC
    y, z = p % NY, p // NY
    px = x % 2
    c64 = c * 64

    def peer_at(dz, dy):
        return (t, wrap(z + dz, NZ) * NY + wrap(y + dy, NY))

    def far_first(i):
        a, b = i // NY, i % NY
        ka, kb = (a + 1) // 2, (b + 1) // 2
        dz = NZ // 2 + ka * (1 - 2 * (a % 2))
        dy = NY // 2 + kb * (1 - 2 * (b % 2))
        return dz, dy

    barrier = pltpu.get_barrier_semaphore()

    close = tuple(peer_at(d, 0) for d in (-1, 1, -2, 2))
    for to in close + tuple(peer_at(0, d) for d in (-1, 1, 2)):
        pl.semaphore_signal(barrier, inc=1, device_id=to, device_id_type=MESH)

    def greet_tower(i, carry):
        pl.semaphore_signal(barrier, inc=1, device_id=(wrap(t + i, NT), p), device_id_type=MESH)
        return carry

    lax.fori_loop(1, NT, greet_tower, 0)

    loads = [
        (w2, W2.at[0, y]), (emb, embv), (lists, listv), (owners, ownv), (counts, cntv), (item, itemv),
    ]
    for s in range(NZ):
        zz = wrap(z + ZREL[s], NZ)
        part = ofv.at[s // 2, :, pl.ds((s % 2) * HZ, HZ)]
        loads.append((of.at[:, pl.ds(pl.multiple_of(zz * HZ, HZ), HZ)], part))
    loads += [(cot, cotv), (ot, otv), (cd, cdv), (cu, cuv), (comp, compv)]
    copies = [pltpu.make_async_copy(a, b, lsem.at[i]) for i, (a, b) in enumerate(loads)]
    for cp in copies:
        cp.start()
    L_W2, L_EMB, L_LIST, L_OWN, L_CNT, L_ITEM, L_OF = 0, 1, 2, 3, 4, 5, 6
    L_COT, L_OT, L_CD, L_CU, L_COMP = 14, 15, 16, 17, 18

    def exchange(src, dst, ssem, rsem):
        def one(i, carry):
            dz, dy = far_first(i)
            to = peer_at(dz, dy)
            pltpu.make_async_remote_copy(
                src_ref=src.at[to[1]], dst_ref=dst.at[p], send_sem=ssem, recv_sem=rsem,
                device_id=to, device_id_type=MESH,
            ).start()
            return carry

        lax.fori_loop(0, NP - 1, one, 0)
        dst[p] = src[p]

    def exchange_wait(dst, sem):
        part = dst.at[pl.ds(0, NP - 1)]
        pltpu.make_async_copy(part, part, sem).wait()

    def towers(src, dst, ssem, rsem):
        for i in range(1, NT):
            to = wrap(t + i, NT)
            pltpu.make_async_remote_copy(
                src_ref=src.at[pl.ds(pl.multiple_of(to * CAP, CAP), CAP)],
                dst_ref=dst.at[pl.ds(pl.multiple_of(t * CAP, CAP), CAP)],
                send_sem=ssem, recv_sem=rsem, device_id=(to, p), device_id_type=MESH,
            ).start()
        mine = pl.ds(pl.multiple_of(t * CAP, CAP), CAP)
        dst[mine] = src[mine]

    def towers_wait(dst, sem):
        part = dst.at[pl.ds(0, SLOTS - CAP)]
        pltpu.make_async_copy(part, part, sem).wait()

    ym, yp, yq = wrap(y - 1, NY), wrap(y + 1, NY), wrap(y + 2, NY)
    SETS = (ym, yp, yq, y)
    near = c64 + px * 32
    other = c64 + (1 - px) * 32
    sent = []

    def start(cp):
        cp.start()
        sent.append(cp)

    def rcopy(src, dst, ssem, rsem, to):
        return pltpu.make_async_remote_copy(
            src_ref=src, dst_ref=dst, send_sem=ssem, recv_sem=rsem, device_id=to, device_id_type=MESH
        )

    def rows(slot, r0, n):
        return W2.at[slot, y, pl.ds(pl.multiple_of(near + r0, 16), n)]

    def rows_b(b, k, r0, n):
        s0, m = BATCH[b]
        return W2.at[pl.ds(s0, m), SETS[k], pl.ds(pl.multiple_of(r0, 16), n)]

    def zc(i):
        a, b, r0, n, d = (
            (0, 2, 0, 32, 1), (0, 3, 0, 32, -1), (0, 4, 0, 32, 2), (0, 5, 0, 32, -2),
            (4, 6, 0, 32, 1), (5, 7, 0, 32, -1), (4, 1, 0, 16, 2), (5, 1, 16, 16, -2),
        )[i]
        return rcopy(rows(a, r0, n), rows(b, r0, n), zs.at[i], zr.at[i], peer_at(d, 0))

    def same(part, ssem, rsem, e, to):
        return rcopy(part, part, ssem.at[e], rsem.at[e], to)

    def y1(b):
        return [same(rows_b(b, 3, near, 32), ys, yr, b * 4 + i, peer_at(0, d)) for i, d in enumerate((1, -1))]

    def y2(b):
        return [same(rows_b(b, i, near + 16 * i, 16), ys, yr, b * 4 + 2 + i, peer_at(0, d)) for i, d in enumerate((1, -1))]

    def xc(b, k):
        return [
            same(rows_b(b, k, near + 16 * i, 16), xs, xr, b * 8 + k * 2 + i, (wrap(x + d, NX) * NC + c, p))
            for i, d in enumerate((1, -1))
        ]

    def dc(b, k, o):
        return same(rows_b(b, k, other if o else near, 32), ds, dr, b * 8 + k * 2 + o, (x * NC + 1 - c, p))

    def own(b):
        for cp in y1(b) + xc(b, 3):
            start(cp)
        start(dc(b, 3, 0))

    def ez(b):
        for i in ((), (0, 1), (2, 3), (4, 5), (6, 7))[b]:
            zc(i).wait_recv()
        if b == 2:
            for i in (4, 5, 6, 7):
                start(zc(i))
        own(b)

    def ey(b):
        for cp in y1(b):
            cp.wait_recv()
        for cp in y2(b) + xc(b, 0) + xc(b, 1):
            start(cp)
        for k in (0, 1):
            start(dc(b, k, 0))

    def ey2(b):
        for cp in y2(b):
            cp.wait_recv()
        for cp in xc(b, 2):
            start(cp)
        start(dc(b, 2, 0))

    def ex(b, *ks):
        for k in ks:
            for cp in xc(b, k):
                cp.wait_recv()
            start(dc(b, k, 1))

    def ed(b):
        for k in range(4 if b else 3):
            for o in (0, 1):
                dc(b, k, o).wait_recv()

    pl.semaphore_wait(barrier, NT - 1 + 7)
    for to in close:
        pl.semaphore_signal(hop1, inc=1, device_id=to, device_id_type=MESH)
    copies[L_W2].wait()
    for i in (0, 1):
        start(zc(i))
    for cp in y1(0):
        start(cp)
    for i in (2, 3):
        start(zc(i))

    copies[L_EMB].wait()
    copies[L_LIST].wait()
    order = listv[...]
    inner = order & (RBLK - 1)
    quarter = order >> 9
    lane = iota((32, 128), 1)

    def build_hot(k, carry):
        r0 = pl.multiple_of(k * 64, 64)
        rows = iota((64, LISTED), 0) + r0
        hot[pl.ds(r0, 64), :] = jnp.where(rows == inner, 1.0, 0.0).astype(BF16)
        return carry

    lax.fori_loop(0, RBLK // 64, build_hot, 0)
    stacked = jnp.concatenate([embv[:, k * RBLK:(k + 1) * RBLK] for k in range(FOLD)], axis=0)
    for n in range(4):
        cols = slice(n * 512, (n + 1) * 512)
        got = dot(stacked, hot[:, cols])
        q = quarter[:, cols]
        srt = jnp.where(q == 0, got[0:64], 0.0)
        for k in range(1, FOLD):
            srt = srt + jnp.where(q == k, got[k * 64:(k + 1) * 64], 0.0)
        for b in range(4):
            blk = srt[:, b * 128:(b + 1) * 128]
            both = jnp.concatenate([blk, pltpu.roll(blk, 96, 1)], axis=0)
            turned = both.T.astype(BF16)
            pay[n * 8 + b * 2] = turned[0:32]
            pay[n * 8 + b * 2 + 1] = turned[64:96]

    pl.semaphore_wait(hop1, 4)
    for to in close[2:]:
        pl.semaphore_signal(hop2, inc=1, device_id=to, device_id_type=MESH)

    copies[L_ITEM].wait()
    for s in range(NZ):
        copies[L_OF + s].wait()

    def item_step(q, carry):
        for h in (slice(0, HZ), slice(HZ, HP)):
            prei[q, :, h] = dot(itemv[...], ofv[q, WIDE:, h])
        return carry

    lax.fori_loop(0, PAIRS // 2, item_step, 0)
    ez(1)
    ey(0)
    lax.fori_loop(PAIRS // 2, PAIRS, item_step, 0)
    ez(2)
    pl.semaphore_wait(hop2, 2)
    exchange(pay, arr, asend, arecv)
    ey2(0)
    ey(1)
    copies[L_COT].wait()
    copies[L_OT].wait()

    def cot_step(n, carry):
        r0 = pl.multiple_of(n * 512, 512)
        g3[:, pl.ds(r0, 512)] = dot_t(cotv[...], otv[pl.ds(r0, 512), :])
        return carry

    lax.fori_loop(0, 2, cot_step, 0)
    ez(3)
    ez(4)
    ey(2)
    ex(1, 3)
    ex(0, 0, 1)

    copies[L_OWN].wait()
    copies[L_CNT].wait()
    own = ownv[...]
    choose = jnp.where(iota((8, UDEV), 0) == own, 1.0, 0.0)
    before = jnp.where(iota((UDEV, UDEV), 0) < iota((UDEV, UDEV), 1), 1.0, 0.0).astype(BF16)
    earlier = dot(choose.astype(BF16), before)
    pos = jnp.sum(choose * earlier, axis=0, keepdims=True)
    target = own * CAP + pos.astype(jnp.int32)
    hit = iota((SLOTS, UDEV), 0) == target
    disp = jnp.where(hit, 1.0, 0.0).astype(BF16)
    held = dot(jnp.where(hit, cntv[...].astype(F32), 0.0).astype(BF16), jnp.ones((UDEV, 128), BF16))
    tsend[:, WIDE:] = held.astype(BF16)
    for i in (L_CD, L_CU, L_COMP):
        copies[i].wait()

    def turn(j, carry):
        at = pl.ds(pl.multiple_of(j * 256, 256), 256)
        cdT[:, at] = cdv[at, :].T
        cuT[at, :] = cuv[:, at].T
        compT[:, at] = compv[at, :].T
        return carry

    lax.fori_loop(0, FEAT // 256, turn, 0)

    exchange_wait(arr, arecv)

    def lay(j, carry):
        a = arr[2 * j].astype(F32)
        b = arr[2 * j + 1].astype(F32)
        at = pl.ds(pl.multiple_of(j * 128, 128), 128)
        SR[0:32, at] = jnp.where(lane < 64, a, pltpu.roll(b, 64, 1)).astype(BF16)
        SR[32:64, at] = jnp.where(lane < 64, pltpu.roll(a, 64, 1), b).astype(BF16)
        return carry

    lax.fori_loop(0, NP // 2, lay, 0)
    low = dot(SR[...], cdv[...]).astype(BF16)
    lift[...] = dot(low, cuv[...])
    wide = SR[...].astype(F32)
    crossed = (wide * lift[...] + wide).astype(BF16)
    compressed = dot(crossed, compv[...]).astype(BF16)
    tsend[:, :WIDE] = dot(disp, compressed).astype(BF16)
    towers(tsend, trecv, tsem, trsem)

    ey2(1)
    ex(2, 3)
    ex(0, 2)
    ey(3)
    ey(4)
    ey2(2)
    ex(1, 0, 1)
    ey2(3)
    ey2(4)
    ex(3, 3)
    ex(4, 3)

    towers_wait(trecv, trsem)
    qi = iota((ROWS, SLOTS), 0)
    si = iota((ROWS, SLOTS), 1) * MOSTC
    spread = jnp.where((qi >= si) & (qi < si + MOSTC), 1.0, 0.0).astype(BF16)
    grid = dot(spread, trecv[...])
    expanded = grid[:, :WIDE].astype(BF16)
    third = (qi * 21846) >> 16
    live = jnp.where((qi - third * MOSTC).astype(F32) < grid[:, WIDE:], 1.0, 0.0)[:, 0:1]

    def first_step(q, carry):
        for h in (slice(0, HZ), slice(HZ, HP)):
            pre = prei[q, :, h] + dot(expanded, ofv[q, :WIDE, h])
            sig = 0.5 * jnp.tanh(0.5 * pre) + 0.5
            act = pre * sig
            hid[q, :, h] = act.astype(BF16)
            slope[q, :, h] = (sig + act * (1.0 - sig)).astype(BF16)
        return carry

    def pair(q):
        return W2[pl.ds(2 * q, 2)].reshape(HP, H2)

    lax.fori_loop(0, PAIRS // 2, first_step, 0)
    ex(1, 2)
    ex(2, 0, 1)
    ex(2, 2)
    lax.fori_loop(PAIRS // 2, PAIRS, first_step, 0)
    ex(3, 0, 1)
    ex(4, 0, 1)
    ed(1)
    pre2[...] = dot(hid[1], pair(1))
    ex(3, 2)
    ex(4, 2)
    ed(2)
    pre2[...] += dot(hid[2], pair(2))
    ed(3)
    pre2[...] += dot(hid[3], pair(3))
    ed(0)
    ed(4)
    pre2[...] += dot(hid[0], pair(0))

    def mid_step(n, carry):
        at = pl.ds(pl.multiple_of(n * 256, 256), 256)
        pre = pre2[:, at]
        sig = 0.5 * jnp.tanh(0.5 * pre) + 0.5
        act = pre * sig
        hs[:, at] = act.astype(BF16)
        gs2[:, at] = (g3[:, at] * live * (sig + act * (1.0 - sig))).astype(BF16)
        return carry

    lax.fori_loop(0, 4, mid_step, 0)

    held_g, acc = None, None
    for q in range(PAIRS):
        d = dot_t(gs2[...], pair(q))
        if q:
            v = dot_t(held_g, ofv[q - 1, :WIDE, :])
            acc = v if acc is None else acc + v
        held_g = (d * slope[q].astype(F32)).astype(BF16)
    acc = acc + dot_t(held_g, ofv[PAIRS - 1, :WIDE, :])
    qj = iota((SLOTS, ROWS), 1)
    sj = iota((SLOTS, ROWS), 0) * MOSTC
    gather3 = jnp.where((qj >= sj) & (qj < sj + MOSTC), 1.0, 0.0).astype(BF16)
    gsend[...] = dot(gather3, acc.astype(BF16)).astype(BF16)
    towers(gsend, grecv, gsem, grsem)

    def out_step(n, carry):
        at = pl.ds(pl.multiple_of(n * 256, 256), 256)
        outv[:, at] = (dot(hs[...], otv[:, at]) * live).astype(BF16)
        return carry

    lax.fori_loop(0, 4, out_step, 0)
    out_copy = pltpu.make_async_copy(outv, out_hbm, lsem.at[19])
    out_copy.start()

    towers_wait(grecv, grsem)
    eye = jnp.where(iota((UDEV, UDEV), 0) == iota((UDEV, UDEV), 1), 1.0, 0.0).astype(BF16)
    undisp = dot_t(eye, disp).astype(BF16)
    session_grad = dot(undisp, grecv[...]).astype(BF16)
    gcv[...] = dot(session_grad, compT[...]).astype(BF16).astype(F32)
    gl = (gcv[...] * SR[...].astype(F32)).astype(BF16)
    glow = dot(gl, cuT[...]).astype(BF16)

    def back_part(i, carry):
        k = (i + 1) // 2
        n = wrap(z // 2 + 2 + k * (1 - 2 * (i % 2)), 4)
        at = pl.ds(pl.multiple_of(n * 512, 512), 512)
        rows_g = gcv[:, at] * (lift[:, at] + 1.0) + dot(glow, cdT[:, at])
        for j in range(4):
            lo = rows_g[0:32, j * 128:(j + 1) * 128]
            hi = rows_g[32:64, j * 128:(j + 1) * 128]
            bpay[n * 8 + 2 * j] = jnp.where(lane < 64, lo, pltpu.roll(hi, 64, 1)).astype(BF16)
            bpay[n * 8 + 2 * j + 1] = jnp.where(lane < 64, pltpu.roll(lo, 64, 1), hi).astype(BF16)
        for e in range(8):
            to = n * 8 + (e % 2) * 4 + wrap(y + (2, 1, 3, 0)[e // 2], NY)

            @pl.when(to != p)
            def _():
                rcopy(bpay.at[to], barr.at[p], bsend, brecv, (t, to)).start()

        return carry

    lax.fori_loop(0, 4, back_part, 0)
    barr[p] = bpay[p]
    for cp in sent:
        cp.wait_send()
    exchange_wait(pay, asend)
    towers_wait(tsend, tsem)
    towers_wait(gsend, gsem)
    exchange_wait(barr, brecv)

    total = jnp.zeros((FOLD * 64, RBLK), F32)
    zero = jnp.zeros((32, 128), F32)
    lane64 = iota((64, 128), 1) & 63
    for n in range(4):
        parts = []
        for b in range(4):
            p0 = n * 8 + b * 2
            tall = jnp.concatenate([barr[p0].astype(F32), zero, barr[p0 + 1].astype(F32), zero], axis=0)
            turned = tall.T
            parts.append(jnp.where(lane64 < 32, turned[0:64], pltpu.roll(turned[64:128], 32, 1)))
        grads = jnp.concatenate(parts, axis=1)
        q = quarter[:, n * 512:(n + 1) * 512]
        laid = jnp.concatenate([jnp.where(q == k, grads, 0.0).astype(BF16) for k in range(FOLD)], axis=0)
        total = total + dot_t(laid, hot[:, n * 512:(n + 1) * 512])
    for k in range(FOLD):
        egv[:, k * RBLK:(k + 1) * RBLK] = total[k * 64:(k + 1) * 64].astype(BF16)
    eg_copy = pltpu.make_async_copy(egv, eg_hbm, lsem.at[20])
    eg_copy.start()
    exchange_wait(bpay, bsend)
    out_copy.wait()
    eg_copy.wait()


def place(a, b, out_a, out_b, held_a, held_b, sem_in, sem_out):
    parts = [(a, held_a, out_a, r0, 96) for r0 in range(0, ROWS, 96)]
    parts += [(b, held_b, out_b, r0, 32) for r0 in (0, 32)]
    first, second = [], []
    for i, (u, h, v, r0, n) in enumerate(parts):
        at = pl.ds(r0, n)
        first.append(pltpu.make_async_copy(u.at[at], h.at[at], sem_in.at[i]))
        second.append(pltpu.make_async_copy(h.at[at], v.at[at], sem_out.at[i]))
    for cp in first:
        cp.start()
    for cp, then in zip(first, second):
        cp.wait()
        then.start()
    for cp in second:
        cp.wait()


def body(
    embeddings, session_lists, owners, counts, item_feats, cotangent,
    cross_down, cross_up, compress, over_first, over_second, over_third,
):
    dma = pltpu.SemaphoreType.DMA
    vm = pltpu.VMEM
    scratch = [
        vm((64, LISTED), BF16), vm((1, LISTED), jnp.int32), vm((1, UDEV), jnp.int32), vm((1, UDEV), jnp.int32),
        vm((ROWS, WIDE), BF16), vm((ROWS, H2), BF16), vm((FEAT, WIDE), BF16), vm((WIDE, FEAT), BF16),
        vm((FEAT, WIDE), BF16), vm((PAIRS, 2 * WIDE, HP), BF16), vm((NZ, NY, HS, H2), BF16), vm((H2, H2), BF16),
        vm((RBLK, LISTED), BF16), vm((NP, 32, 128), BF16), vm((NP, 32, 128), BF16), vm((UDEV, FEAT), BF16),
        vm((UDEV, FEAT), F32), vm((SLOTS, WIDE + 128), BF16), vm((SLOTS, WIDE + 128), BF16),
        vm((SLOTS, WIDE), BF16), vm((SLOTS, WIDE), BF16), vm((NP, 32, 128), BF16), vm((NP, 32, 128), BF16),
        vm((64, LISTED), BF16),
        vm((PAIRS, ROWS, HP), F32), vm((PAIRS, ROWS, HP), BF16), vm((PAIRS, ROWS, HP), BF16), vm((ROWS, H2), F32),
        vm((ROWS, H2), F32), vm((ROWS, H2), BF16), vm((ROWS, H2), BF16), vm((ROWS, H2), BF16), vm((WIDE, FEAT), BF16),
        vm((FEAT, WIDE), BF16), vm((WIDE, FEAT), BF16), vm((UDEV, FEAT), F32),
        dma((21,)), dma, dma, dma, dma, dma, dma, dma, dma,
        dma((8,)), dma((8,)), dma((20,)), dma((20,)), dma((40,)), dma((40,)), dma((40,)), dma((40,)),
        pltpu.SemaphoreType.REGULAR, pltpu.SemaphoreType.REGULAR,
    ]
    anywhere = pl.BlockSpec(memory_space=pl.ANY)
    over_out, emb_grad_t = pl.pallas_call(
        kernel,
        out_shape=(
            jax.ShapeDtypeStruct((ROWS, H2), BF16),
            jax.ShapeDtypeStruct((64, LISTED), BF16),
        ),
        in_specs=[anywhere] * 12,
        out_specs=(anywhere, anywhere),
        scratch_shapes=scratch,
        compiler_params=pltpu.CompilerParams(
            collective_id=0, has_side_effects=True, vmem_limit_bytes=60 * 2**20
        ),
    )(
        embeddings.T, session_lists, owners.reshape(1, UDEV), counts.reshape(1, UDEV), item_feats, cotangent,
        cross_down, cross_up, compress, over_first, over_second, over_third,
    )
    over_out, emb_grad_t = pl.pallas_call(
        place,
        out_shape=(
            jax.ShapeDtypeStruct((ROWS, H2), BF16),
            jax.ShapeDtypeStruct((64, LISTED), BF16),
        ),
        in_specs=[anywhere] * 2,
        out_specs=(anywhere, anywhere),
        scratch_shapes=[vm((ROWS, H2), BF16), vm((64, LISTED), BF16), dma((6,)), dma((6,))],
        compiler_params=pltpu.CompilerParams(vmem_limit_bytes=60 * 2**20),
    )(over_out, emb_grad_t)
    return over_out, emb_grad_t.T


def solution(mesh):
    return jax.shard_map(
        body,
        mesh=mesh,
        in_specs=(
            P("tower", "peer"),
            P("tower", None),
            P(("tower", "peer"), None),
            P(("tower", "peer")),
            P(("tower", "peer"), None),
            P(("tower", "peer"), None),
            P(),
            P(),
            P(),
            P(),
            P("peer", None),
            P(),
        ),
        out_specs=(P(("tower", "peer"), None), P("tower", "peer")),
        check_vma=False,
    )
```

```python
import jax
import jax.numpy as jnp
from jax import lax
from jax.experimental import pallas as pl
from jax.experimental.pallas import tpu as pltpu
from jax.sharding import PartitionSpec as P

MESH = pl.DeviceIdType.MESH
F32 = jnp.float32
BF16 = jnp.bfloat16
NX, NC, NY, NZ = 4, 2, 4, 8
NP, NT = NY * NZ, NX * NC
ROWS, SLOTS, MOSTC, CAP = 384, 128, 3, 16
UDEV = 64
FEAT, WIDE = 2048, 256
H1, H2 = 4096, 1024
HZ = H1 // NZ
HS = H1 // NP
LISTED = UDEV * NP
FOLD = 4
RBLK = LISTED // FOLD
ZREL = (0, 4, 7, 1, 6, 2, 5, 3)
BATCH = ((0, 1), (2, 2), (4, 2), (6, 2), (1, 1))
PAIRS = NZ // 2
HP = 2 * HZ


def dot(a, b):
    return jnp.dot(a, b, preferred_element_type=F32)


def dot_t(a, b):
    return lax.dot_general(a, b, (((1,), (1,)), ((), ())), preferred_element_type=F32)


def wrap(v, n):
    return lax.rem(v + 2 * n, n)


def iota(shape, axis):
    return lax.broadcasted_iota(jnp.int32, shape, axis)


def kernel(
    emb, lists, owners, counts, item, cot, cd, cu, comp, of, w2, ot,
    out_hbm, eg_hbm,
    embv, listv, ownv, cntv, itemv, cotv, cdv, cuv, compv, ofv, W2, otv,
    hot, pay, arr, SR, lift, tsend, trecv, gsend, grecv, bpay, barr, egv,
    prei, hid, slope, pre2, g3, hs, gs2, outv, cdT, cuT, compT, gcv,
    lsem, asend, arecv, tsem, trsem, gsem, grsem, bsend, brecv,
    zs, zr, ys, yr, xs, xr, ds, dr, hop1, hop2,
):
    t = lax.axis_index("tower")
    p = lax.axis_index("peer")
    x, c = t // NC, t % NC
    y, z = p % NY, p // NY
    px = x % 2
    c64 = c * 64

    def peer_at(dz, dy):
        return (t, wrap(z + dz, NZ) * NY + wrap(y + dy, NY))

    def far_first(i):
        a, b = i // NY, i % NY
        ka, kb = (a + 1) // 2, (b + 1) // 2
        dz = NZ // 2 + ka * (1 - 2 * (a % 2))
        dy = NY // 2 + kb * (1 - 2 * (b % 2))
        return dz, dy

    barrier = pltpu.get_barrier_semaphore()

    close = tuple(peer_at(d, 0) for d in (-1, 1, -2, 2))
    for to in close + tuple(peer_at(0, d) for d in (-1, 1, 2)):
        pl.semaphore_signal(barrier, inc=1, device_id=to, device_id_type=MESH)

    def greet_tower(i, carry):
        pl.semaphore_signal(barrier, inc=1, device_id=(wrap(t + i, NT), p), device_id_type=MESH)
        return carry

    lax.fori_loop(1, NT, greet_tower, 0)

    loads = [
        (w2, W2.at[0, y]), (emb, embv), (lists, listv), (owners, ownv), (counts, cntv), (item, itemv),
    ]
    for s in range(NZ):
        zz = wrap(z + ZREL[s], NZ)
        part = ofv.at[s // 2, :, pl.ds((s % 2) * HZ, HZ)]
        loads.append((of.at[:, pl.ds(pl.multiple_of(zz * HZ, HZ), HZ)], part))
    loads += [(cot, cotv), (ot, otv), (cd, cdv), (cu, cuv), (comp, compv)]
    copies = [pltpu.make_async_copy(a, b, lsem.at[i]) for i, (a, b) in enumerate(loads)]
    for cp in copies:
        cp.start()
    L_W2, L_EMB, L_LIST, L_OWN, L_CNT, L_ITEM, L_OF = 0, 1, 2, 3, 4, 5, 6
    L_COT, L_OT, L_CD, L_CU, L_COMP = 14, 15, 16, 17, 18

    def exchange(src, dst, ssem, rsem):
        def one(i, carry):
            dz, dy = far_first(i)
            to = peer_at(dz, dy)
            pltpu.make_async_remote_copy(
                src_ref=src.at[to[1]], dst_ref=dst.at[p], send_sem=ssem, recv_sem=rsem,
                device_id=to, device_id_type=MESH,
            ).start()
            return carry

        lax.fori_loop(0, NP - 1, one, 0)
        dst[p] = src[p]

    def exchange_wait(dst, sem):
        part = dst.at[pl.ds(0, NP - 1)]
        pltpu.make_async_copy(part, part, sem).wait()

    def towers(src, dst, ssem, rsem):
        for i in range(1, NT):
            to = wrap(t + i, NT)
            pltpu.make_async_remote_copy(
                src_ref=src.at[pl.ds(pl.multiple_of(to * CAP, CAP), CAP)],
                dst_ref=dst.at[pl.ds(pl.multiple_of(t * CAP, CAP), CAP)],
                send_sem=ssem, recv_sem=rsem, device_id=(to, p), device_id_type=MESH,
            ).start()
        mine = pl.ds(pl.multiple_of(t * CAP, CAP), CAP)
        dst[mine] = src[mine]

    def towers_wait(dst, sem):
        part = dst.at[pl.ds(0, SLOTS - CAP)]
        pltpu.make_async_copy(part, part, sem).wait()

    ym, yp, yq = wrap(y - 1, NY), wrap(y + 1, NY), wrap(y + 2, NY)
    SETS = (ym, yp, yq, y)
    near = c64 + px * 32
    other = c64 + (1 - px) * 32
    sent = []

    def start(cp):
        cp.start()
        sent.append(cp)

    def rcopy(src, dst, ssem, rsem, to):
        return pltpu.make_async_remote_copy(
            src_ref=src, dst_ref=dst, send_sem=ssem, recv_sem=rsem, device_id=to, device_id_type=MESH
        )

    def rows(slot, r0, n):
        return W2.at[slot, y, pl.ds(pl.multiple_of(near + r0, 16), n)]

    def rows_b(b, k, r0, n):
        s0, m = BATCH[b]
        return W2.at[pl.ds(s0, m), SETS[k], pl.ds(pl.multiple_of(r0, 16), n)]

    def zc(i):
        a, b, r0, n, d = (
            (0, 2, 0, 32, 1), (0, 3, 0, 32, -1), (0, 4, 0, 32, 2), (0, 5, 0, 32, -2),
            (4, 6, 0, 32, 1), (5, 7, 0, 32, -1), (4, 1, 0, 16, 2), (5, 1, 16, 16, -2),
        )[i]
        return rcopy(rows(a, r0, n), rows(b, r0, n), zs.at[i], zr.at[i], peer_at(d, 0))

    def same(part, ssem, rsem, e, to):
        return rcopy(part, part, ssem.at[e], rsem.at[e], to)

    def y1(b):
        return [same(rows_b(b, 3, near, 32), ys, yr, b * 4 + i, peer_at(0, d)) for i, d in enumerate((1, -1))]

    def y2(b):
        return [same(rows_b(b, i, near + 16 * i, 16), ys, yr, b * 4 + 2 + i, peer_at(0, d)) for i, d in enumerate((1, -1))]

    def xc(b, k):
        return [
            same(rows_b(b, k, near + 16 * i, 16), xs, xr, b * 8 + k * 2 + i, (wrap(x + d, NX) * NC + c, p))
            for i, d in enumerate((1, -1))
        ]

    def dc(b, k, o):
        return same(rows_b(b, k, other if o else near, 32), ds, dr, b * 8 + k * 2 + o, (x * NC + 1 - c, p))

    def own(b):
        for cp in y1(b) + xc(b, 3):
            start(cp)
        start(dc(b, 3, 0))

    def ez(b):
        for i in ((), (0, 1), (2, 3), (4, 5), (6, 7))[b]:
            zc(i).wait_recv()
        if b == 2:
            for i in (4, 5, 6, 7):
                start(zc(i))
        own(b)

    def ey(b):
        for cp in y1(b):
            cp.wait_recv()
        for cp in y2(b) + xc(b, 0) + xc(b, 1):
            start(cp)
        for k in (0, 1):
            start(dc(b, k, 0))

    def ey2(b):
        for cp in y2(b):
            cp.wait_recv()
        for cp in xc(b, 2):
            start(cp)
        start(dc(b, 2, 0))

    def ex(b, *ks):
        for k in ks:
            for cp in xc(b, k):
                cp.wait_recv()
            start(dc(b, k, 1))

    def ed(b):
        for k in range(4 if b else 3):
            for o in (0, 1):
                dc(b, k, o).wait_recv()

    pl.semaphore_wait(barrier, NT - 1 + 7)
    for to in close:
        pl.semaphore_signal(hop1, inc=1, device_id=to, device_id_type=MESH)
    copies[L_W2].wait()
    for i in (0, 1):
        start(zc(i))
    for cp in y1(0):
        start(cp)
    for i in (2, 3):
        start(zc(i))

    copies[L_EMB].wait()
    copies[L_LIST].wait()
    order = listv[...]
    inner = order & (RBLK - 1)
    quarter = order >> 9
    lane = iota((32, 128), 1)

    def build_hot(k, carry):
        r0 = pl.multiple_of(k * 64, 64)
        rows = iota((64, LISTED), 0) + r0
        hot[pl.ds(r0, 64), :] = jnp.where(rows == inner, 1.0, 0.0).astype(BF16)
        return carry

    lax.fori_loop(0, RBLK // 64, build_hot, 0)
    stacked = jnp.concatenate([embv[:, k * RBLK:(k + 1) * RBLK] for k in range(FOLD)], axis=0)
    for n in range(4):
        cols = slice(n * 512, (n + 1) * 512)
        got = dot(stacked, hot[:, cols])
        q = quarter[:, cols]
        srt = jnp.where(q == 0, got[0:64], 0.0)
        for k in range(1, FOLD):
            srt = srt + jnp.where(q == k, got[k * 64:(k + 1) * 64], 0.0)
        for b in range(4):
            blk = srt[:, b * 128:(b + 1) * 128]
            both = jnp.concatenate([blk, pltpu.roll(blk, 96, 1)], axis=0)
            turned = both.T.astype(BF16)
            pay[n * 8 + b * 2] = turned[0:32]
            pay[n * 8 + b * 2 + 1] = turned[64:96]

    pl.semaphore_wait(hop1, 4)
    for to in close[2:]:
        pl.semaphore_signal(hop2, inc=1, device_id=to, device_id_type=MESH)

    copies[L_ITEM].wait()
    for s in range(NZ):
        copies[L_OF + s].wait()

    def item_step(q, carry):
        for h in (slice(0, HZ), slice(HZ, HP)):
            prei[q, :, h] = dot(itemv[...], ofv[q, WIDE:, h])
        return carry

    lax.fori_loop(0, PAIRS // 2, item_step, 0)
    ez(1)
    ey(0)
    lax.fori_loop(PAIRS // 2, PAIRS, item_step, 0)
    ez(2)
    pl.semaphore_wait(hop2, 2)
    exchange(pay, arr, asend, arecv)
    ey2(0)
    ey(1)
    copies[L_COT].wait()
    copies[L_OT].wait()

    def cot_step(n, carry):
        r0 = pl.multiple_of(n * 512, 512)
        g3[:, pl.ds(r0, 512)] = dot_t(cotv[...], otv[pl.ds(r0, 512), :])
        return carry

    lax.fori_loop(0, 2, cot_step, 0)
    ez(3)
    ez(4)
    ey(2)
    ex(1, 3)
    ex(0, 0, 1)

    copies[L_OWN].wait()
    copies[L_CNT].wait()
    own = ownv[...]
    choose = jnp.where(iota((8, UDEV), 0) == own, 1.0, 0.0)
    before = jnp.where(iota((UDEV, UDEV), 0) < iota((UDEV, UDEV), 1), 1.0, 0.0).astype(BF16)
    earlier = dot(choose.astype(BF16), before)
    pos = jnp.sum(choose * earlier, axis=0, keepdims=True)
    target = own * CAP + pos.astype(jnp.int32)
    hit = iota((SLOTS, UDEV), 0) == target
    disp = jnp.where(hit, 1.0, 0.0).astype(BF16)
    held = dot(jnp.where(hit, cntv[...].astype(F32), 0.0).astype(BF16), jnp.ones((UDEV, 128), BF16))
    tsend[:, WIDE:] = held.astype(BF16)
    for i in (L_CD, L_CU, L_COMP):
        copies[i].wait()

    def turn(j, carry):
        at = pl.ds(pl.multiple_of(j * 256, 256), 256)
        cdT[:, at] = cdv[at, :].T
        cuT[at, :] = cuv[:, at].T
        compT[:, at] = compv[at, :].T
        return carry

    lax.fori_loop(0, FEAT // 256, turn, 0)

    exchange_wait(arr, arecv)

    def lay(j, carry):
        a = arr[2 * j].astype(F32)
        b = arr[2 * j + 1].astype(F32)
        at = pl.ds(pl.multiple_of(j * 128, 128), 128)
        SR[0:32, at] = jnp.where(lane < 64, a, pltpu.roll(b, 64, 1)).astype(BF16)
        SR[32:64, at] = jnp.where(lane < 64, pltpu.roll(a, 64, 1), b).astype(BF16)
        return carry

    lax.fori_loop(0, NP // 2, lay, 0)
    low = dot(SR[...], cdv[...]).astype(BF16)
    lift[...] = dot(low, cuv[...])
    wide = SR[...].astype(F32)
    crossed = (wide * lift[...] + wide).astype(BF16)
    compressed = dot(crossed, compv[...]).astype(BF16)
    tsend[:, :WIDE] = dot(disp, compressed).astype(BF16)
    towers(tsend, trecv, tsem, trsem)

    ey2(1)
    ex(2, 3)
    ex(0, 2)
    ey(3)
    ey(4)
    ey2(2)
    ex(1, 0, 1)
    ey2(3)
    ey2(4)
    ex(3, 3)
    ex(4, 3)

    towers_wait(trecv, trsem)
    qi = iota((ROWS, SLOTS), 0)
    si = iota((ROWS, SLOTS), 1) * MOSTC
    spread = jnp.where((qi >= si) & (qi < si + MOSTC), 1.0, 0.0).astype(BF16)
    grid = dot(spread, trecv[...])
    expanded = grid[:, :WIDE].astype(BF16)
    third = (qi * 21846) >> 16
    live = jnp.where((qi - third * MOSTC).astype(F32) < grid[:, WIDE:], 1.0, 0.0)[:, 0:1]

    def first_step(q, carry):
        for h in (slice(0, HZ), slice(HZ, HP)):
            pre = prei[q, :, h] + dot(expanded, ofv[q, :WIDE, h])
            sig = 0.5 * jnp.tanh(0.5 * pre) + 0.5
            act = pre * sig
            hid[q, :, h] = act.astype(BF16)
            slope[q, :, h] = (sig + act * (1.0 - sig)).astype(BF16)
        return carry

    def pair(q):
        return W2[pl.ds(2 * q, 2)].reshape(HP, H2)

    lax.fori_loop(0, PAIRS // 2, first_step, 0)
    ex(1, 2)
    ex(2, 0, 1)
    ex(2, 2)
    lax.fori_loop(PAIRS // 2, PAIRS, first_step, 0)
    ex(3, 0, 1)
    ex(4, 0, 1)
    ed(0)
    pre2[...] = dot(hid[0, :, :HZ], W2[0].reshape(HZ, H2))
    ex(3, 2)
    ex(4, 2)
    ed(1)
    pre2[...] += dot(hid[1], pair(1))
    ed(2)
    pre2[...] += dot(hid[2], pair(2))
    ed(3)
    pre2[...] += dot(hid[3], pair(3))
    ed(4)
    pre2[...] += dot(hid[0, :, HZ:], W2[1].reshape(HZ, H2))

    def mid_step(n, carry):
        at = pl.ds(pl.multiple_of(n * 256, 256), 256)
        pre = pre2[:, at]
        sig = 0.5 * jnp.tanh(0.5 * pre) + 0.5
        act = pre * sig
        hs[:, at] = act.astype(BF16)
        gs2[:, at] = (g3[:, at] * live * (sig + act * (1.0 - sig))).astype(BF16)
        return carry

    lax.fori_loop(0, 4, mid_step, 0)

    held_g, acc = None, None
    for q in range(PAIRS):
        d = dot_t(gs2[...], pair(q))
        if q:
            v = dot_t(held_g, ofv[q - 1, :WIDE, :])
            acc = v if acc is None else acc + v
        held_g = (d * slope[q].astype(F32)).astype(BF16)
    acc = acc + dot_t(held_g, ofv[PAIRS - 1, :WIDE, :])
    qj = iota((SLOTS, ROWS), 1)
    sj = iota((SLOTS, ROWS), 0) * MOSTC
    gather3 = jnp.where((qj >= sj) & (qj < sj + MOSTC), 1.0, 0.0).astype(BF16)
    gsend[...] = dot(gather3, acc.astype(BF16)).astype(BF16)
    towers(gsend, grecv, gsem, grsem)

    def out_step(n, carry):
        at = pl.ds(pl.multiple_of(n * 256, 256), 256)
        outv[:, at] = (dot(hs[...], otv[:, at]) * live).astype(BF16)
        return carry

    lax.fori_loop(0, 4, out_step, 0)
    out_copy = pltpu.make_async_copy(outv, out_hbm, lsem.at[19])
    out_copy.start()

    towers_wait(grecv, grsem)
    eye = jnp.where(iota((UDEV, UDEV), 0) == iota((UDEV, UDEV), 1), 1.0, 0.0).astype(BF16)
    undisp = dot_t(eye, disp).astype(BF16)
    session_grad = dot(undisp, grecv[...]).astype(BF16)
    gcv[...] = dot(session_grad, compT[...]).astype(BF16).astype(F32)
    gl = (gcv[...] * SR[...].astype(F32)).astype(BF16)
    glow = dot(gl, cuT[...]).astype(BF16)

    def back_part(i, carry):
        k = (i + 1) // 2
        n = wrap(z // 2 + 2 + k * (1 - 2 * (i % 2)), 4)
        at = pl.ds(pl.multiple_of(n * 512, 512), 512)
        rows_g = gcv[:, at] * (lift[:, at] + 1.0) + dot(glow, cdT[:, at])
        for j in range(4):
            lo = rows_g[0:32, j * 128:(j + 1) * 128]
            hi = rows_g[32:64, j * 128:(j + 1) * 128]
            bpay[n * 8 + 2 * j] = jnp.where(lane < 64, lo, pltpu.roll(hi, 64, 1)).astype(BF16)
            bpay[n * 8 + 2 * j + 1] = jnp.where(lane < 64, pltpu.roll(lo, 64, 1), hi).astype(BF16)
        for e in range(8):
            to = n * 8 + (e % 2) * 4 + wrap(y + (2, 1, 3, 0)[e // 2], NY)

            @pl.when(to != p)
            def _():
                rcopy(bpay.at[to], barr.at[p], bsend, brecv, (t, to)).start()

        return carry

    lax.fori_loop(0, 4, back_part, 0)
    barr[p] = bpay[p]
    for cp in sent:
        cp.wait_send()
    exchange_wait(pay, asend)
    towers_wait(tsend, tsem)
    towers_wait(gsend, gsem)
    exchange_wait(barr, brecv)

    total = jnp.zeros((FOLD * 64, RBLK), F32)
    zero = jnp.zeros((32, 128), F32)
    lane64 = iota((64, 128), 1) & 63
    for n in range(4):
        parts = []
        for b in range(4):
            p0 = n * 8 + b * 2
            tall = jnp.concatenate([barr[p0].astype(F32), zero, barr[p0 + 1].astype(F32), zero], axis=0)
            turned = tall.T
            parts.append(jnp.where(lane64 < 32, turned[0:64], pltpu.roll(turned[64:128], 32, 1)))
        grads = jnp.concatenate(parts, axis=1)
        q = quarter[:, n * 512:(n + 1) * 512]
        laid = jnp.concatenate([jnp.where(q == k, grads, 0.0).astype(BF16) for k in range(FOLD)], axis=0)
        total = total + dot_t(laid, hot[:, n * 512:(n + 1) * 512])
    for k in range(FOLD):
        egv[:, k * RBLK:(k + 1) * RBLK] = total[k * 64:(k + 1) * 64].astype(BF16)
    eg_copy = pltpu.make_async_copy(egv, eg_hbm, lsem.at[20])
    eg_copy.start()
    exchange_wait(bpay, bsend)
    out_copy.wait()
    eg_copy.wait()


def place(a, b, out_a, out_b, held_a, held_b, sem_in, sem_out):
    parts = [(a, held_a, out_a, r0, 96) for r0 in range(0, ROWS, 96)]
    parts += [(b, held_b, out_b, r0, 32) for r0 in (0, 32)]
    first, second = [], []
    for i, (u, h, v, r0, n) in enumerate(parts):
        at = pl.ds(r0, n)
        first.append(pltpu.make_async_copy(u.at[at], h.at[at], sem_in.at[i]))
        second.append(pltpu.make_async_copy(h.at[at], v.at[at], sem_out.at[i]))
    for cp in first:
        cp.start()
    for cp, then in zip(first, second):
        cp.wait()
        then.start()
    for cp in second:
        cp.wait()


def body(
    embeddings, session_lists, owners, counts, item_feats, cotangent,
    cross_down, cross_up, compress, over_first, over_second, over_third,
):
    dma = pltpu.SemaphoreType.DMA
    vm = pltpu.VMEM
    scratch = [
        vm((64, LISTED), BF16), vm((1, LISTED), jnp.int32), vm((1, UDEV), jnp.int32), vm((1, UDEV), jnp.int32),
        vm((ROWS, WIDE), BF16), vm((ROWS, H2), BF16), vm((FEAT, WIDE), BF16), vm((WIDE, FEAT), BF16),
        vm((FEAT, WIDE), BF16), vm((PAIRS, 2 * WIDE, HP), BF16), vm((NZ, NY, HS, H2), BF16), vm((H2, H2), BF16),
        vm((RBLK, LISTED), BF16), vm((NP, 32, 128), BF16), vm((NP, 32, 128), BF16), vm((UDEV, FEAT), BF16),
        vm((UDEV, FEAT), F32), vm((SLOTS, WIDE + 128), BF16), vm((SLOTS, WIDE + 128), BF16),
        vm((SLOTS, WIDE), BF16), vm((SLOTS, WIDE), BF16), vm((NP, 32, 128), BF16), vm((NP, 32, 128), BF16),
        vm((64, LISTED), BF16),
        vm((PAIRS, ROWS, HP), F32), vm((PAIRS, ROWS, HP), BF16), vm((PAIRS, ROWS, HP), BF16), vm((ROWS, H2), F32),
        vm((ROWS, H2), F32), vm((ROWS, H2), BF16), vm((ROWS, H2), BF16), vm((ROWS, H2), BF16), vm((WIDE, FEAT), BF16),
        vm((FEAT, WIDE), BF16), vm((WIDE, FEAT), BF16), vm((UDEV, FEAT), F32),
        dma((21,)), dma, dma, dma, dma, dma, dma, dma, dma,
        dma((8,)), dma((8,)), dma((20,)), dma((20,)), dma((40,)), dma((40,)), dma((40,)), dma((40,)),
        pltpu.SemaphoreType.REGULAR, pltpu.SemaphoreType.REGULAR,
    ]
    anywhere = pl.BlockSpec(memory_space=pl.ANY)
    over_out, emb_grad_t = pl.pallas_call(
        kernel,
        out_shape=(
            jax.ShapeDtypeStruct((ROWS, H2), BF16),
            jax.ShapeDtypeStruct((64, LISTED), BF16),
        ),
        in_specs=[anywhere] * 12,
        out_specs=(anywhere, anywhere),
        scratch_shapes=scratch,
        compiler_params=pltpu.CompilerParams(
            collective_id=0, has_side_effects=True, vmem_limit_bytes=60 * 2**20
        ),
    )(
        embeddings.T, session_lists, owners.reshape(1, UDEV), counts.reshape(1, UDEV), item_feats, cotangent,
        cross_down, cross_up, compress, over_first, over_second, over_third,
    )
    over_out, emb_grad_t = pl.pallas_call(
        place,
        out_shape=(
            jax.ShapeDtypeStruct((ROWS, H2), BF16),
            jax.ShapeDtypeStruct((64, LISTED), BF16),
        ),
        in_specs=[anywhere] * 2,
        out_specs=(anywhere, anywhere),
        scratch_shapes=[vm((ROWS, H2), BF16), vm((64, LISTED), BF16), dma((6,)), dma((6,))],
        compiler_params=pltpu.CompilerParams(vmem_limit_bytes=60 * 2**20),
    )(over_out, emb_grad_t)
    return over_out, emb_grad_t.T


def solution(mesh):
    return jax.shard_map(
        body,
        mesh=mesh,
        in_specs=(
            P("tower", "peer"),
            P("tower", None),
            P(("tower", "peer"), None),
            P(("tower", "peer")),
            P(("tower", "peer"), None),
            P(("tower", "peer"), None),
            P(),
            P(),
            P(),
            P(),
            P("peer", None),
            P(),
        ),
        out_specs=(P(("tower", "peer"), None), P("tower", "peer")),
        check_vma=False,
    )
```
